1024 devices in a mesh: rep: 16 (over x, y_hi), exp: 64 (over y_lo, z, core).
Axes of the slice: x: 4, y: 8 (y_hi: 4, y_lo: 2; y = y_hi * 2 + y_lo), z: 16, core: 2. Of those that a mesh axis runs over, the one named last changes fastest.
Arguments:
- quant_rows: bfloat16 [32768, 2048], P(('rep', 'exp')), may hold values from -6 to 6
- row_scales: bfloat16 [32768], P(('rep', 'exp')), may hold values from 0.29882812 to 3
- out_grads: bfloat16 [32768, 2048], P(('rep', 'exp')), may hold values from -6 to 6
- routes: int32 [32768, 4], P(('rep', 'exp')), may hold values from 0 to 63, all different within a row; in each aligned block of 32 rows (0 to 31, 32 to 63, ...) at most 4 rows name the same one
- probs: bfloat16 [32768, 4], P(('rep', 'exp')), may hold values from 0.099609375 to 1
- w_gate: bfloat16 [64, 2048, 768], P('exp'), may hold values from -0.125 to 0.125
- w_up: bfloat16 [64, 2048, 768], P('exp'), may hold values from -0.125 to 0.125
- w_down: bfloat16 [64, 768, 2048], P('exp'), may hold values from -0.21875 to 0.21875
Outputs:
- input_grads: bfloat16 [32768, 2048], P(('rep', 'exp'))
- grad_gate: bfloat16 [64, 2048, 768], P('exp', 'rep')
- grad_up: bfloat16 [64, 2048, 768], P('exp', 'rep')
The draws below stay inside these ranges and needn't reach their ends.
Inputs may be any that keep to these rules, and one draw needn't show every extreme that they name: `routes`: each token names 4 different experts; among the tokens of one device no expert is named more than 4 times, a bound that some block reaches.
All inputs are finite; a program needn't handle non-finite values.
Results may differ from the reference program's by a relative error of at most 0.018.
Values may be sent and summed in bfloat16 or wider, within the bound.
A program may use at most 128 MiB of HBM per device.

```python
import math
import jax
import jax.numpy as jnp
import numpy as np
from jax import lax

D = 2048
FF = 768
TOP = 4
TOK_DEV = 32
EXPERTS = 64
CAP = 4
TOKENS = 32768
N_REP = 16
N_EXP = 64


def block_scale(own_key, extent, pieces, smallest, high):
    gain = 1.0
    for dim, shards_of in pieces:
        steps = jax.random.uniform(jax.random.fold_in(jax.random.fold_in(own_key, 6), dim), (shards_of,), jnp.float32, smallest / len(pieces), high / len(pieces))
        gain = gain * jnp.repeat(jnp.exp(steps), extent[dim] // shards_of).reshape((-1,) + (1,) * (len(extent) - 1 - dim))
    return gain


def routed_block(own_key, own, number, rows, amount, top, most, skew):
    order = jax.random.permutation(own_key, amount)
    crowded, common = load_shares(amount, rows * top, most, skew, True), load_shares(amount, rows * top, most, skew, False)
    places = jnp.arange(amount)

    def named(lengths, rotation):
        used = int((lengths > 0).sum())
        fixed = max(1, used // 4)
        passed = fixed + (places - fixed + rotation * (used - fixed)) % max(1, amount - fixed)
        return jnp.zeros((amount,), jnp.int32).at[order[jnp.where(places < fixed, places, passed)]].set(jnp.asarray(lengths, jnp.int32))

    lengths = jnp.where(number % 4 == 0, named(crowded, number // 4), named(common, number - number // 4 - 1))
    mixed = jax.random.permutation(jax.random.fold_in(own, 3), amount)
    donor, receiver = mixed[0:amount // 2 * 2:2], mixed[1:amount // 2 * 2:2]
    slack = jnp.minimum(lengths[donor] - 1, most - lengths[receiver]) // 2
    slack = jnp.where((donor == order[0]) | (receiver == order[0]) | (lengths[receiver] == 0), 0, jnp.maximum(slack, 0))
    passed = jax.random.randint(jax.random.fold_in(own, 4), (amount // 2,), 0, 1 << 20) % (slack + 1)
    lengths = lengths.at[donor].add(-passed).at[receiver].add(passed)
    members = jnp.searchsorted(jnp.cumsum(lengths), jnp.arange(rows * top), side="right").astype(jnp.int32)
    grid = members.reshape(top, rows).T
    grid = grid[jax.random.permutation(jax.random.fold_in(own, 1), rows)]
    rotation = jax.random.randint(jax.random.fold_in(own, 2), (rows, 1), 0, top)
    return jnp.take_along_axis(grid, (jnp.arange(top)[None, :] + rotation) % top, axis=1)


def load_shares(amount, total, most, skew, full):
    weights = [(1 << 20) // math.isqrt(rank ** skew) + 1 for rank in range(1, amount + 1)]
    largest = most if full else min(most, max(-(-total // amount), total * weights[0] // sum(weights)))
    least = 1 if total - largest >= amount - 1 else 0
    holding, rest = [largest] + [least] * (amount - 1), total - largest - least * (amount - 1)
    while rest > 0:
        candidates = [i for i in range(1, amount) if holding[i] < largest] or [i for i in range(1, amount) if holding[i] < most]
        mass, budget = sum([weights[i] for i in candidates]), rest
        for i in candidates:
            addition = min(most - holding[i], max(1, budget * weights[i] // mass), rest)
            holding[i] = holding[i] + addition
            rest = rest - addition
    return np.array(holding)


def bell_draw(stream_key, shape, spread, most, split=(), kind=jnp.bfloat16):
    factor_of = block_scale(stream_key, shape, split, -0.22, 0.18) if split else 1.0
    result = jax.random.normal(stream_key, shape, jnp.float32) * spread * factor_of
    return jnp.minimum(jnp.maximum(result, -most), most).astype(kind)


def setup_inputs(seed: int = 0) -> dict:
    streams_of = jax.random.split(jax.random.key(seed), 9)
    quant_rows = bell_draw(streams_of[0], (TOKENS, D), 1.0, 6.0, ((0, 1024),))
    row_scales = jnp.clip(jnp.exp(math.log(3.0) - 2.306499 * jax.random.uniform(streams_of[1], (TOKENS,), jnp.float32) ** block_scale(streams_of[1], (TOKENS,), ((0, 1024),), -0.2, 0.2)), 0.29882812, 3.0).astype(jnp.bfloat16)
    out_grads = bell_draw(streams_of[2], (TOKENS, D), 1.0, 6.0, ((0, 1024),))
    routes_keys = jax.random.split(jax.random.fold_in(streams_of[3], 1), TOKENS // TOK_DEV)
    routes_turns = jax.random.permutation(jax.random.fold_in(streams_of[3], 3), TOKENS // TOK_DEV)
    routes = jax.vmap(lambda own, number: routed_block(jax.random.fold_in(streams_of[3], 2), own, number, TOK_DEV, EXPERTS, TOP, CAP, 2))(routes_keys, routes_turns).reshape((TOKENS, TOP))
    probs = jnp.clip(jnp.exp(math.log(1.0) - 2.306499 * jax.random.uniform(streams_of[4], (TOKENS, TOP), jnp.float32) ** block_scale(streams_of[4], (TOKENS, TOP), ((0, 1024),), -0.2, 0.2)), 0.099609375, 1.0).astype(jnp.bfloat16)
    w_gate = bell_draw(streams_of[5], (EXPERTS, D, FF), D ** -0.5, 0.125, ((0, 64),))
    w_up = bell_draw(streams_of[6], (EXPERTS, D, FF), D ** -0.5, 0.125, ((0, 64),))
    w_down = bell_draw(streams_of[7], (EXPERTS, FF, D), FF ** -0.5, 0.21875, ((0, 64),))
    return dict(quant_rows=quant_rows, row_scales=row_scales, out_grads=out_grads, routes=routes, probs=probs, w_gate=w_gate, w_up=w_up, w_down=w_down)


def swiglu_backward(gate_proj, up_proj, grad_hidden):
    sigmoid_gate = jax.nn.sigmoid(gate_proj)
    act_slope = sigmoid_gate * (1.0 + gate_proj * (1.0 - sigmoid_gate))
    gate_grad = (grad_hidden * up_proj * act_slope).astype(jnp.bfloat16)
    up_grad = (grad_hidden * gate_proj * sigmoid_gate).astype(jnp.bfloat16)
    return gate_grad, up_grad


def reference(quant_rows, row_scales, out_grads, routes, probs, w_gate, w_up, w_down):
    token_rows = quant_rows.reshape(N_REP, N_EXP, TOK_DEV, D)
    grad_rows = out_grads.reshape(N_REP, N_EXP, TOK_DEV, D)
    scale_rows = row_scales.reshape(N_REP, N_EXP, TOK_DEV)
    route_rows = routes.reshape(N_REP, N_EXP, TOK_DEV * TOP)
    prob_rows = probs.reshape(N_REP, N_EXP, TOK_DEV * TOP)
    source_ids = jnp.arange(N_EXP, dtype=jnp.int32)[:, None]

    def one_group(weight_sum, inputs):
        tokens_here, grads_here, scales_here, routes_here, probs_here = inputs
        chosen = (routes_here[:, :, None] == jnp.arange(EXPERTS, dtype=jnp.int32)[None, None, :]).astype(jnp.int32)
        earlier = jnp.cumsum(chosen, axis=1) - chosen
        slot_rank = jnp.sum(earlier * chosen, axis=2)
        target = routes_here * CAP + slot_rank
        route_ids = jnp.broadcast_to(jnp.arange(TOK_DEV * TOP, dtype=jnp.int32)[None, :], (N_EXP, TOK_DEV * TOP))
        table = jnp.full((N_EXP, EXPERTS * CAP), -1, jnp.int32).at[source_ids, target].set(route_ids)
        per_expert = table.reshape(N_EXP, EXPERTS, CAP).transpose(1, 0, 2)

        def one_expert(expert_inputs):
            route_index, gate_weight, up_weight, down_weight = expert_inputs
            valid = route_index >= 0
            safe_index = jnp.maximum(route_index, 0)
            token_index = safe_index // TOP
            rows_x = tokens_here[source_ids, token_index].reshape(N_EXP * CAP, D)
            rows_g = grads_here[source_ids, token_index].reshape(N_EXP * CAP, D)
            scale_col = jnp.where(valid, scales_here[source_ids, token_index].astype(jnp.float32), 0.0).reshape(N_EXP * CAP, 1)
            prob_col = jnp.where(valid, probs_here[source_ids, safe_index].astype(jnp.float32), 0.0).reshape(N_EXP * CAP, 1)
            gate_proj = jnp.dot(rows_x, gate_weight, preferred_element_type=jnp.float32) * scale_col
            up_proj = jnp.dot(rows_x, up_weight, preferred_element_type=jnp.float32) * scale_col
            grad_hidden = jnp.dot(rows_g, down_weight.T, preferred_element_type=jnp.float32) * prob_col
            gate_grad, up_grad = swiglu_backward(gate_proj, up_proj, grad_hidden)
            row_grads = jnp.dot(gate_grad, gate_weight.T, preferred_element_type=jnp.float32)
            row_grads = (row_grads + jnp.dot(up_grad, up_weight.T, preferred_element_type=jnp.float32)).astype(jnp.bfloat16)
            scaled_rows = (rows_x.astype(jnp.float32) * scale_col).astype(jnp.bfloat16)
            both_grads = jnp.concatenate([gate_grad, up_grad], axis=1)
            partial_sum = jnp.dot(scaled_rows.T, both_grads, preferred_element_type=jnp.float32).astype(jnp.bfloat16)
            partial_sum = lax.optimization_barrier(partial_sum)
            return row_grads.reshape(N_EXP, CAP, D), partial_sum

        row_grads, partials = lax.map(one_expert, (per_expert, w_gate, w_up, w_down))
        valid_all = per_expert >= 0
        token_all = jnp.maximum(per_expert, 0) // TOP
        source_all = jnp.broadcast_to(jnp.arange(N_EXP, dtype=jnp.int32)[None, :, None], per_expert.shape)
        row_values = jnp.where(valid_all[..., None], row_grads.astype(jnp.float32), 0.0)
        input_sum = jnp.zeros((N_EXP, TOK_DEV, D), jnp.float32).at[source_all, token_all].add(row_values)
        return weight_sum + partials.astype(jnp.float32), input_sum.astype(jnp.bfloat16)

    start_sum = jnp.zeros((EXPERTS, D, 2 * FF), jnp.float32)
    weight_sum, input_grads = lax.scan(one_group, start_sum, (token_rows, grad_rows, scale_rows, route_rows, prob_rows))
    weights_out = weight_sum.astype(jnp.bfloat16)
    return input_grads.reshape(TOKENS, D), weights_out[:, :, :FF], weights_out[:, :, FF:]
```

```python
import functools

import jax
import jax.numpy as jnp
from jax import lax
from jax.experimental import pallas as pl
from jax.experimental.pallas import tpu as pltpu
from jax.sharding import PartitionSpec as P

MESH = pl.DeviceIdType.MESH
F32 = jnp.float32
BF16 = jnp.bfloat16

NX, NYH, NZ, NC = 4, 4, 16, 2
NJ = 4
HALF = NZ // 2
CAP = 4
SUBS = 3


def kernel(
    x_ref, scale_ref, g_ref, routes_ref, probs_ref, wg_hbm, wu_hbm, wd_hbm,
    out_ref, gate_ref, up_ref,
    wg, wu, wd, meta, xs, gs, pm, stage, got, xt, both, rows_back, returned, yown,
    zsend, zrecv, dw, zed, recv1, recv2,
    w_sem, f_send, f_recv, p_send, p_recv, b_send, b_recv, z_send, z_recv, r_send, r_recv,
):
    tok, dim = x_ref.shape
    ff = wg.shape[1]
    tile = 256
    pieces = 2 * ff // tile
    rep, exp = lax.axis_index("rep"), lax.axis_index("exp")
    my_x, my_y = rep // NYH, rep % NYH
    y_lo, z, core = exp // (NZ * NC), exp // NC % NZ, exp % NC

    def z_dev(step):
        return (rep, y_lo * (NZ * NC) + (z + NZ + step) % NZ * NC + core)

    def plane_exp(j):
        other_y = 1 - y_lo if j // 2 else y_lo
        other_c = 1 - core if j % 2 else core
        return other_y * (NZ * NC) + z * NC + other_c

    def x_dev(step):
        return ((my_x + NX + step) % NX * NYH + my_y, exp)

    def y_dev(step):
        return (my_x * NYH + (my_y + NYH + step) % NYH, exp)

    weights = [
        pltpu.make_async_copy(src, dst, w_sem.at[i])
        for i, (src, dst) in enumerate(((wg_hbm, wg), (wu_hbm, wu), (wd_hbm, wd)))
    ]
    for copy in weights:
        copy.start()

    neighbours = [z_dev(1), z_dev(-1), x_dev(1), x_dev(-1), y_dev(1), y_dev(-1)]
    neighbours += [(rep, plane_exp(j)) for j in range(1, NJ)]
    barrier = pltpu.get_barrier_semaphore()
    for device in neighbours:
        pl.semaphore_signal(barrier, inc=1, device_id=device, device_id_type=MESH)

    def iota(shape, axis):
        return lax.broadcasted_iota(jnp.int32, shape, axis)

    diag = jnp.where(iota((tok, tok), 0) == iota((tok, tok), 1), scale_ref[...].astype(F32), 0.0)
    diag = diag.astype(BF16)
    xs[0] = jnp.dot(diag, x_ref[...], preferred_element_type=F32).astype(BF16)
    gs[0] = g_ref[...]
    lanes = NJ * tok
    spread = (iota((tok, lanes), 1) % tok == iota((tok, lanes), 0)).astype(BF16)
    over_tokens = (((0,), (0,)), ((), ()))
    table = lax.dot_general(
        routes_ref[...].astype(F32).astype(BF16), spread, over_tokens, preferred_element_type=F32
    )
    chance = lax.dot_general(probs_ref[...], spread, over_tokens, preferred_element_type=F32)
    experts = NJ * NZ
    hits = [iota((experts, lanes), 0).astype(F32) == table[k : k + 1] for k in range(4)]
    named = sum(hit.astype(F32) for hit in hits)
    a, b = iota((lanes, lanes), 0), iota((lanes, lanes), 1)
    before = ((a // tok == b // tok) & (a < b)).astype(BF16)
    rank = jnp.dot(named.astype(BF16), before, preferred_element_type=F32)
    for k in range(4):
        mine = jnp.sum(jnp.where(hits[k], rank, 0.0), axis=0, keepdims=True)
        meta[0, k : k + 1, :] = table[k : k + 1] * CAP + mine
        meta[0, 4 + k : 5 + k, :] = chance[k : k + 1]

    pl.semaphore_wait(barrier, len(neighbours))

    pending = []

    def remote(src, dst, send, recv, device):
        return pltpu.make_async_remote_copy(
            src_ref=src, dst_ref=dst, send_sem=send, recv_sem=recv,
            device_id=device, device_id_type=MESH,
        )

    travels = (meta, xs, gs)

    def slot_of(way, hop):
        return 0 if hop == 0 else 15 if hop == HALF else 2 * hop - 1 + way

    def carries(way, hop, sub):
        return hop < HALF or (sub == 2) == (way == 1)

    def hop_copy(way, hop, sub):
        buf = travels[sub]
        return remote(
            buf.at[slot_of(way, hop - 1)], buf.at[slot_of(way, hop)],
            f_send.at[way, hop - 1, sub], f_recv.at[way, hop - 1, sub],
            z_dev(1 if way == 0 else -1),
        )

    def hop_start(way, hop, sub):
        if hop <= HALF and carries(way, hop, sub):
            copy = hop_copy(way, hop, sub)
            copy.start()
            pending.append(copy)

    for sub in range(SUBS):
        for way in range(2):
            hop_start(way, 1, sub)

    group_rows = NJ * 4 * CAP
    r = iota((group_rows, lanes), 0)
    c = iota((group_rows, lanes), 1)
    expert_of = jnp.where(
        r // 16 == 0, plane_exp(0),
        jnp.where(r // 16 == 1, plane_exp(1), jnp.where(r // 16 == 2, plane_exp(2), plane_exp(3))),
    )
    slot_id = jnp.where(r % 16 // CAP == c // tok, expert_of * CAP + r % CAP, -1).astype(F32)

    def plane_copy(group, j, kind):
        return remote(
            stage.at[kind, group, j], got.at[kind, j, pl.ds(group * 16, 16)],
            p_send.at[group, j - 1, kind], p_recv.at[group, j - 1, kind], (rep, plane_exp(j)),
        )

    def select(group):
        lane_group = iota((8, lanes), 1) // tok
        mix = meta[group * 4]
        for m in range(1, 4):
            mix = jnp.where(lane_group == m, meta[group * 4 + m], mix)
        hit = [slot_id == mix[k : k + 1] for k in range(4)]
        ones = sum(h.astype(F32) for h in hit)
        pm[group] = ones.astype(BF16)
        weighed = sum(jnp.where(hit[k], mix[4 + k : 5 + k], 0.0) for k in range(4))
        picks = (pm[group], weighed.astype(BF16))
        for kind, buf in ((0, xs), (1, gs)):
            for n in range(0, dim, 512):
                block = buf[group * 4 : group * 4 + 4, :, n : n + 512].reshape(4 * tok, 512)
                chosen = jnp.dot(picks[kind], block, preferred_element_type=F32).astype(BF16)
                got[kind, 0, group * 16 : group * 16 + 16, n : n + 512] = chosen[:16]
                stage[kind, group, 1:, :, n : n + 512] = chosen[16:].reshape(3, 16, 512)
            for j in range(1, NJ):
                copy = plane_copy(group, j, kind)
                copy.start()
                pending.append(copy)

    for hop in range(1, HALF + 1):
        for sub in range(SUBS):
            for way in range(2):
                if carries(way, hop, sub):
                    hop_copy(way, hop, sub).wait_recv()
                    hop_start(way, hop + 1, sub)
        if hop % 2 == 0:
            select(hop // 2 - 1)

    for copy in weights:
        copy.wait()
    for group in range(4):
        for j in range(1, NJ):
            for kind in range(2):
                plane_copy(group, j, kind).wait_recv()

    slots = NJ * 64
    over_last = (((1,), (1,)), ((), ()))

    def project(f, carry):
        cols = pl.ds(pl.multiple_of(f * tile, tile), tile)
        ins = got[0].reshape(slots, dim)
        gate = jnp.dot(ins, wg[:, cols], preferred_element_type=F32)
        up = jnp.dot(ins, wu[:, cols], preferred_element_type=F32)
        grads = got[1].reshape(slots, dim)
        hidden = lax.dot_general(grads, wd[cols, :], over_last, preferred_element_type=F32)
        s = jax.nn.sigmoid(gate)
        both[f] = (hidden * up * s * (1.0 + gate * (1.0 - s))).astype(BF16)
        both[f + ff // tile] = (hidden * gate * s).astype(BF16)
        return carry

    lax.fori_loop(0, ff // tile, project, 0)

    def turn(n, carry):
        cols = pl.ds(pl.multiple_of(n * tile, tile), tile)
        xt[n] = got[0, :, :, cols].reshape(slots, tile).T
        return carry

    lax.fori_loop(0, dim // tile, turn, 0)

    axes = ((x_dev, y_dev), (y_dev, x_dev))
    order_of = [1 if p == 1 else 0 for p in range(pieces)]

    def weight_piece(p):
        order = order_of[p]

        def one(i, carry):
            value = jnp.dot(xt[i], both[p], preferred_element_type=F32).astype(BF16)
            rx = (i // 2 - my_x + NX) % NX
            for h in range(2):
                ry = (2 * (i % 2) + h - my_y + NYH) % NYH
                part = value[h * 128 : (h + 1) * 128]
                if order == 0:
                    dw[p, rx, ry] = part
                else:
                    dw[p, ry, rx] = part
            return carry

        lax.fori_loop(0, dim // tile, one, 0)

    def ring_copy(phase, p, way, m):
        to = axes[order_of[p]][phase](1 if way == 0 else -1)
        near = 1 if way == 0 else 3
        block = (2, near, near)[m]
        half = (way, 1 - way, way)[m]
        if phase == 0:
            src = dw.at[p, block, pl.ds(half * 2, 2)]
            dst = recv1.at[p, way, m]
        else:
            src = zed.at[p, block, pl.ds(half * 64, 64)]
            dst = recv2.at[p, way, m]
        return remote(src, dst, r_send.at[phase, p, way, m], r_recv.at[phase, p, way, m], to)

    def ring_start(phase, p, way, m):
        copy = ring_copy(phase, p, way, m)
        copy.start()
        pending.append(copy)

    def ring_first(phase, p):
        for m in range(2):
            for way in range(2):
                ring_start(phase, p, way, m)

    def ring_add(phase, p):
        for way in range(2):
            ring_copy(phase, p, way, 0).wait_recv()
            near = 1 if way == 0 else 3
            if phase == 0:
                for h in range(2):
                    dw[p, near, way * 2 + h] = (
                        dw[p, near, way * 2 + h].astype(F32) + recv1[p, way, 0, h].astype(F32)
                    ).astype(BF16)
            else:
                here = pl.ds(way * 64, 64)
                zed[p, near, here] = (
                    zed[p, near, here].astype(F32) + recv2[p, way, 0].astype(F32)
                ).astype(BF16)
            ring_start(phase, p, way, 2)

    def ring_end(phase, p):
        for way in range(2):
            for m in range(1, 3):
                ring_copy(phase, p, way, m).wait_recv()
        for half in range(2):
            low_m, high_m = (2, 1) if half == 0 else (1, 2)
            if phase == 0:
                for h in range(2):
                    total = dw[p, 0, half * 2 + h].astype(F32)
                    total += recv1[p, 0, low_m, h].astype(F32)
                    total += recv1[p, 1, high_m, h].astype(F32)
                    zed[p, half * 2 + h] = total.astype(BF16)
            else:
                here = pl.ds(half * 64, 64)
                total = zed[p, 0, here].astype(F32)
                total += recv2[p, 0, low_m].astype(F32)
                total += recv2[p, 1, high_m].astype(F32)
                target = gate_ref if p < pieces // 2 else up_ref
                q = p % (pieces // 2)
                target[here, q * tile : (q + 1) * tile] = total.astype(BF16)
        if phase == 0:
            ring_first(1, p)

    def back_copy(j):
        return remote(
            rows_back.at[j], returned.at[j], b_send.at[j - 1], b_recv.at[j - 1],
            (rep, plane_exp(j)),
        )

    def row_grads():
        def one(n, carry):
            cols = pl.ds(pl.multiple_of(n * tile, tile), tile)
            total = jnp.zeros((slots, tile), F32)
            for k in range(ff // tile):
                inner = slice(k * tile, (k + 1) * tile)
                total += lax.dot_general(
                    both[k], wg[cols, inner], over_last, preferred_element_type=F32
                )
                total += lax.dot_general(
                    both[k + ff // tile], wu[cols, inner], over_last, preferred_element_type=F32
                )
            value = total.astype(BF16).reshape(NJ, 64, tile)
            rows_back[:, :, cols] = value
            return carry

        lax.fori_loop(0, dim // tile, one, 0)
        for j in range(1, NJ):
            copy = back_copy(j)
            copy.start()
            pending.append(copy)

    def combine():
        for j in range(1, NJ):
            back_copy(j).wait_recv()
        for group in range(3, -1, -1):
            rows = pl.ds(group * 16, 16)
            for n in range(0, dim, 512):
                cols = slice(n, n + 512)
                parts = jnp.concatenate(
                    [rows_back[0, rows, cols]] + [returned[j, rows, cols] for j in range(1, NJ)], 0
                )
                sums = lax.dot_general(pm[group], parts, over_tokens, preferred_element_type=F32)
                yown[group * 4 : group * 4 + 4, :, cols] = sums.reshape(4, tok, 512)

    wide = dim // 2

    def line_copy(way, hop, half):
        return remote(
            zsend.at[way, hop - 1, half], zrecv.at[way, hop - 1, half],
            z_send.at[way, hop - 1, half], z_recv.at[way, hop - 1, half],
            z_dev(-1 if way == 0 else 1),
        )

    def line_start(way, hop, half):
        copy = line_copy(way, hop, half)
        copy.start()
        pending.append(copy)

    def line_far():
        for way in range(2):
            zsend[way, HALF - 1, way] = yown[15, :, way * wide : (way + 1) * wide].astype(BF16)
            line_start(way, HALF, way)

    def line_step(hop):
        halves = ((1, 0), (0, 1)) if hop == HALF - 1 else ((0, 1), (0, 1))
        for turn_ in range(2):
            for way in range(2):
                half = halves[way][turn_] if hop == HALF - 1 else turn_
                total = yown[slot_of(way, hop), :, half * wide : (half + 1) * wide]
                if hop < HALF - 1 or half == way:
                    line_copy(way, hop + 1, half).wait_recv()
                    total = total + zrecv[way, hop, half].astype(F32)
                zsend[way, hop - 1, half] = total.astype(BF16)
                line_start(way, hop, half)

    def line_end():
        for half in range(2):
            cols = slice(half * wide, (half + 1) * wide)
            total = yown[0, :, cols]
            for way in range(2):
                line_copy(way, 1, half).wait_recv()
                total = total + zrecv[way, 0, half].astype(F32)
            out_ref[:, cols] = total.astype(BF16)

    tasks = []
    weight_piece(0)
    ring_first(0, 0)
    weight_piece(1)
    ring_first(0, 1)
    row_grads()
    weight_piece(2)
    ring_first(0, 2)
    for p in range(3, pieces):
        weight_piece(p)

    x_pieces = [p for p in range(pieces) if order_of[p] == 0]
    y_pieces = [p for p in range(pieces) if order_of[p] == 1]

    def lot(p, follow):
        ring_add(0, p)
        if follow is not None:
            ring_first(0, follow)

    step = 7.9
    for i, p in enumerate(x_pieces):
        follow = x_pieces[i + 2] if i + 2 < len(x_pieces) else None
        tasks.append((step * i + 4, functools.partial(lot, p, follow)))
        tasks.append((step * (i + 1) + 2, functools.partial(ring_end, 0, p)))
        tasks.append((step * (i + 1) + 5, functools.partial(ring_add, 1, p)))
        tasks.append((step * (i + 1) + 9, functools.partial(ring_end, 1, p)))
    for i, p in enumerate(y_pieces):
        tasks.append((8.5, functools.partial(ring_add, 0, p)))
        tasks.append((24, functools.partial(ring_end, 0, p)))
        tasks.append((29, functools.partial(ring_add, 1, p)))
        tasks.append((33, functools.partial(ring_end, 1, p)))
    tasks.append((11, combine))
    tasks.append((11.1, line_far))
    for hop in range(HALF - 1, 0, -1):
        tasks.append((11.2 + 3.5 * (HALF - hop), functools.partial(line_step, hop)))
    tasks.append((11.2 + 3.5 * HALF, line_end))
    for _, task in sorted(tasks, key=lambda entry: entry[0]):
        task()
    for copy in pending:
        copy.wait_send()


def body(quant_rows, row_scales, out_grads, routes, probs, w_gate, w_up, w_down):
    tok, dim = quant_rows.shape
    ff = w_gate.shape[2]
    pieces = 2 * ff // 256
    vmem = pl.BlockSpec(memory_space=pltpu.VMEM)
    hbm = pl.BlockSpec(memory_space=pl.ANY)
    dma = pltpu.SemaphoreType.DMA
    wide = dim // 2
    out, gate, up = pl.pallas_call(
        kernel,
        out_shape=(
            jax.ShapeDtypeStruct((tok, dim), BF16),
            jax.ShapeDtypeStruct((128, ff), BF16),
            jax.ShapeDtypeStruct((128, ff), BF16),
        ),
        in_specs=[vmem] * 5 + [hbm] * 3,
        out_specs=(vmem, vmem, vmem),
        scratch_shapes=[
            pltpu.VMEM((dim, ff), BF16),
            pltpu.VMEM((dim, ff), BF16),
            pltpu.VMEM((ff, dim), BF16),
            pltpu.VMEM((NZ, 8, NJ * tok), F32),
            pltpu.VMEM((NZ, tok, dim), BF16),
            pltpu.VMEM((NZ, tok, dim), BF16),
            pltpu.VMEM((4, 64, NJ * tok), BF16),
            pltpu.VMEM((2, 4, NJ, 16, dim), BF16),
            pltpu.VMEM((2, NJ, 64, dim), BF16),
            pltpu.VMEM((dim // 256, 256, 256), BF16),
            pltpu.VMEM((pieces, 256, 256), BF16),
            pltpu.VMEM((NJ, 64, dim), BF16),
            pltpu.VMEM((NJ, 64, dim), BF16),
            pltpu.VMEM((NZ, tok, dim), F32),
            pltpu.VMEM((2, HALF, 2, tok, wide), BF16),
            pltpu.VMEM((2, HALF, 2, tok, wide), BF16),
            pltpu.VMEM((pieces, 4, 4, 128, 256), BF16),
            pltpu.VMEM((pieces, 4, 128, 256), BF16),
            pltpu.VMEM((pieces, 2, 3, 2, 128, 256), BF16),
            pltpu.VMEM((pieces, 2, 3, 64, 256), BF16),
            dma((3,)),
            dma((2, HALF, SUBS)),
            dma((2, HALF, SUBS)),
            dma((4, 3, 2)),
            dma((4, 3, 2)),
            dma((3,)),
            dma((3,)),
            dma((2, HALF, 2)),
            dma((2, HALF, 2)),
            dma((2, pieces, 2, 3)),
            dma((2, pieces, 2, 3)),
        ],
        compiler_params=pltpu.CompilerParams(
            collective_id=0, has_side_effects=True, vmem_limit_bytes=60 * 1024 * 1024
        ),
    )(
        quant_rows, row_scales.reshape(1, tok), out_grads, routes, probs,
        w_gate[0], w_up[0], w_down[0],
    )
    return out, gate[None], up[None]


def solution(mesh):
    in_specs = (
        P(("rep", "exp"), None),
        P(("rep", "exp")),
        P(("rep", "exp"), None),
        P(("rep", "exp"), None),
        P(("rep", "exp"), None),
        P("exp", None, None),
        P("exp", None, None),
        P("exp", None, None),
    )
    out_specs = (P(("rep", "exp"), None), P("exp", "rep", None), P("exp", "rep", None))
    return jax.shard_map(body, mesh=mesh, in_specs=in_specs, out_specs=out_specs, check_vma=False)
```

```python
import functools

import jax
import jax.numpy as jnp
from jax import lax
from jax.experimental import pallas as pl
from jax.experimental.pallas import tpu as pltpu
from jax.sharding import PartitionSpec as P

MESH = pl.DeviceIdType.MESH
F32 = jnp.float32
BF16 = jnp.bfloat16

NX, NYH, NZ, NC = 4, 4, 16, 2
NJ = 4
HALF = NZ // 2
CAP = 4
SUBS = 3


def kernel(
    x_ref, scale_ref, g_ref, routes_ref, probs_ref, wg_hbm, wu_hbm, wd_hbm,
    out_ref, gate_ref, up_ref,
    wg, wu, wd, meta, xs, gs, pm, stage, got, xt, both, rows_back, returned, yown,
    zsend, zrecv, dw, zed, recv1, recv2,
    w_sem, f_send, f_recv, p_send, p_recv, b_send, b_recv, z_send, z_recv, r_send, r_recv,
):
    tok, dim = x_ref.shape
    ff = wg.shape[1]
    tile = 256
    pieces = 2 * ff // tile
    rep, exp = lax.axis_index("rep"), lax.axis_index("exp")
    my_x, my_y = rep // NYH, rep % NYH
    y_lo, z, core = exp // (NZ * NC), exp // NC % NZ, exp % NC

    def z_dev(step):
        return (rep, y_lo * (NZ * NC) + (z + NZ + step) % NZ * NC + core)

    def plane_exp(j):
        other_y = 1 - y_lo if j // 2 else y_lo
        other_c = 1 - core if j % 2 else core
        return other_y * (NZ * NC) + z * NC + other_c

    def x_dev(step):
        return ((my_x + NX + step) % NX * NYH + my_y, exp)

    def y_dev(step):
        return (my_x * NYH + (my_y + NYH + step) % NYH, exp)

    weights = [
        pltpu.make_async_copy(src, dst, w_sem.at[i])
        for i, (src, dst) in enumerate(((wg_hbm, wg), (wu_hbm, wu), (wd_hbm, wd)))
    ]
    for copy in weights:
        copy.start()

    neighbours = [z_dev(1), z_dev(-1), x_dev(1), x_dev(-1), y_dev(1), y_dev(-1)]
    neighbours += [(rep, plane_exp(j)) for j in range(1, NJ)]
    barrier = pltpu.get_barrier_semaphore()
    for device in neighbours:
        pl.semaphore_signal(barrier, inc=1, device_id=device, device_id_type=MESH)

    def iota(shape, axis):
        return lax.broadcasted_iota(jnp.int32, shape, axis)

    diag = jnp.where(iota((tok, tok), 0) == iota((tok, tok), 1), scale_ref[...].astype(F32), 0.0)
    diag = diag.astype(BF16)
    xs[0] = jnp.dot(diag, x_ref[...], preferred_element_type=F32).astype(BF16)
    gs[0] = g_ref[...]
    lanes = NJ * tok
    spread = (iota((tok, lanes), 1) % tok == iota((tok, lanes), 0)).astype(BF16)
    over_tokens = (((0,), (0,)), ((), ()))
    table = jnp.dot(
        routes_ref[...].astype(F32).astype(BF16), spread, preferred_element_type=F32
    )
    chance = jnp.dot(probs_ref[...], spread, preferred_element_type=F32)
    experts = NJ * NZ
    hits = [iota((experts, lanes), 0).astype(F32) == table[k : k + 1] for k in range(4)]
    named = sum(hit.astype(F32) for hit in hits)
    a, b = iota((lanes, lanes), 0), iota((lanes, lanes), 1)
    before = ((a // tok == b // tok) & (a < b)).astype(BF16)
    rank = jnp.dot(named.astype(BF16), before, preferred_element_type=F32)
    for k in range(4):
        mine = jnp.sum(jnp.where(hits[k], rank, 0.0), axis=0, keepdims=True)
        meta[0, k : k + 1, :] = table[k : k + 1] * CAP + mine
        meta[0, 4 + k : 5 + k, :] = chance[k : k + 1]

    pl.semaphore_wait(barrier, len(neighbours))

    pending = []

    def remote(src, dst, send, recv, device):
        return pltpu.make_async_remote_copy(
            src_ref=src, dst_ref=dst, send_sem=send, recv_sem=recv,
            device_id=device, device_id_type=MESH,
        )

    travels = (meta, xs, gs)

    def slot_of(way, hop):
        return 0 if hop == 0 else 15 if hop == HALF else 2 * hop - 1 + way

    def carries(way, hop, sub):
        return hop < HALF or (sub == 2) == (way == 1)

    def hop_copy(way, hop, sub):
        buf = travels[sub]
        return remote(
            buf.at[slot_of(way, hop - 1)], buf.at[slot_of(way, hop)],
            f_send.at[way, hop - 1, sub], f_recv.at[way, hop - 1, sub],
            z_dev(1 if way == 0 else -1),
        )

    def hop_start(way, hop, sub):
        if hop <= HALF and carries(way, hop, sub):
            copy = hop_copy(way, hop, sub)
            copy.start()
            pending.append(copy)

    for sub in range(SUBS):
        for way in range(2):
            hop_start(way, 1, sub)

    group_rows = NJ * 4 * CAP
    r = iota((group_rows, lanes), 0)
    c = iota((group_rows, lanes), 1)
    expert_of = jnp.where(
        r // 16 == 0, plane_exp(0),
        jnp.where(r // 16 == 1, plane_exp(1), jnp.where(r // 16 == 2, plane_exp(2), plane_exp(3))),
    )
    slot_id = jnp.where(r % 16 // CAP == c // tok, expert_of * CAP + r % CAP, -1).astype(F32)

    def plane_copy(group, j, kind):
        return remote(
            stage.at[kind, group, j], got.at[kind, group, j],
            p_send.at[group, j - 1, kind], p_recv.at[group, j - 1, kind], (rep, plane_exp(j)),
        )

    def select(group):
        lane_group = iota((8, lanes), 1) // tok
        mix = meta[group * 4]
        for m in range(1, 4):
            mix = jnp.where(lane_group == m, meta[group * 4 + m], mix)
        hit = [slot_id == mix[k : k + 1] for k in range(4)]
        ones = sum(h.astype(F32) for h in hit)
        pm[group] = ones.astype(BF16)
        weighed = sum(jnp.where(hit[k], mix[4 + k : 5 + k], 0.0) for k in range(4))
        picks = (pm[group], weighed.astype(BF16))
        for kind, buf in ((0, xs), (1, gs)):
            for n in range(0, dim, 512):
                block = buf[group * 4 : group * 4 + 4, :, n : n + 512].reshape(4 * tok, 512)
                chosen = jnp.dot(picks[kind], block, preferred_element_type=F32).astype(BF16)
                got[kind, group, 0, :, n : n + 512] = chosen[:16]
                stage[kind, group, 1:, :, n : n + 512] = chosen[16:].reshape(3, 16, 512)
            for j in range(1, NJ):
                copy = plane_copy(group, j, kind)
                copy.start()
                pending.append(copy)

    slots = NJ * 64
    over_last = (((1,), (1,)), ((), ()))

    def project(low, high):
        for group in range(low, high):
            for j in range(1, NJ):
                for kind in range(2):
                    plane_copy(group, j, kind).wait_recv()
        here, count = slice(low * 64, high * 64), (high - low) * 64
        for f in range(ff // tile):
            cols = slice(f * tile, (f + 1) * tile)
            ins = got[0, low:high].reshape(count, dim)
            gate = jnp.dot(ins, wg[:, cols], preferred_element_type=F32)
            up = jnp.dot(ins, wu[:, cols], preferred_element_type=F32)
            grads = got[1, low:high].reshape(count, dim)
            hidden = lax.dot_general(grads, wd[cols, :], over_last, preferred_element_type=F32)
            s = jax.nn.sigmoid(gate)
            both[f, here] = (hidden * up * s * (1.0 + gate * (1.0 - s))).astype(BF16)
            both[f + ff // tile, here] = (hidden * gate * s).astype(BF16)
        for n in range(dim // tile):
            block = got[0, low:high, :, :, n * tile : (n + 1) * tile]
            xt[n, :, here] = block.reshape(count, tile).T

    def back_copy(part, j):
        rows = pl.ds(0, 48) if part == 0 else pl.ds(48, 16)
        return remote(
            rows_back.at[j, rows], returned.at[j, rows],
            b_send.at[part, j - 1], b_recv.at[part, j - 1], (rep, plane_exp(j)),
        )

    def row_grads(part):
        low, high = ((0, 3), (3, 4))[part]
        here, count = slice(low * 64, high * 64), (high - low) * 64

        def one(n, carry):
            cols = pl.ds(pl.multiple_of(n * tile, tile), tile)
            total = jnp.zeros((count, tile), F32)
            for k in range(ff // tile):
                inner = slice(k * tile, (k + 1) * tile)
                total += lax.dot_general(
                    both[k, here], wg[cols, inner], over_last, preferred_element_type=F32
                )
                total += lax.dot_general(
                    both[k + ff // tile, here], wu[cols, inner], over_last,
                    preferred_element_type=F32,
                )
            value = total.astype(BF16).reshape(high - low, NJ, 16, tile)
            for j in range(NJ):
                rows = slice(low * 16, high * 16)
                rows_back[j, rows, cols] = value[:, j].reshape(count // NJ, tile)
            return carry

        lax.fori_loop(0, dim // tile, one, 0)

    def back_start(part):
        for j in range(1, NJ):
            copy = back_copy(part, j)
            copy.start()
            pending.append(copy)

    for hop in range(1, HALF + 1):
        for sub in range(SUBS):
            for way in range(2):
                if carries(way, hop, sub):
                    hop_copy(way, hop, sub).wait_recv()
                    hop_start(way, hop + 1, sub)
        if hop == 2:
            for copy in weights:
                copy.wait()
        if hop % 2 == 0:
            select(hop // 2 - 1)
        elif hop == 5:
            project(0, 2)
    project(2, 3)
    row_grads(0)
    project(3, 4)

    axes = ((x_dev, y_dev), (y_dev, x_dev))
    order_of = [1 if p == 1 else 0 for p in range(pieces)]

    def weight_piece(p):
        order = order_of[p]

        for i in range(dim // tile):
            value = jnp.dot(xt[i], both[p], preferred_element_type=F32).astype(BF16)
            rx = (i // 2 - my_x + NX) % NX
            for h in range(2):
                ry = (2 * (i % 2) + h - my_y + NYH) % NYH
                part = value[h * 128 : (h + 1) * 128]
                if order == 0:
                    dw[p, rx, ry] = part
                else:
                    dw[p, ry, rx] = part

    def ring_copy(phase, p, way, m):
        to = axes[order_of[p]][phase](1 if way == 0 else -1)
        near = 1 if way == 0 else 3
        block = (2, near, near)[m]
        half = (way, 1 - way, way)[m]
        if phase == 0:
            src = dw.at[p, block, pl.ds(half * 2, 2)]
            dst = recv1.at[p, way, m]
        else:
            src = zed.at[p, block, pl.ds(half * 64, 64)]
            dst = recv2.at[p, way, m]
        return remote(src, dst, r_send.at[phase, p, way, m], r_recv.at[phase, p, way, m], to)

    def ring_start(phase, p, way, m):
        copy = ring_copy(phase, p, way, m)
        copy.start()
        pending.append(copy)

    def ring_first(phase, p):
        for m in range(2):
            for way in range(2):
                ring_start(phase, p, way, m)

    def ring_add(phase, p):
        for way in range(2):
            ring_copy(phase, p, way, 0).wait_recv()
            near = 1 if way == 0 else 3
            if phase == 0:
                for h in range(2):
                    dw[p, near, way * 2 + h] = (
                        dw[p, near, way * 2 + h].astype(F32) + recv1[p, way, 0, h].astype(F32)
                    ).astype(BF16)
            else:
                here = pl.ds(way * 64, 64)
                zed[p, near, here] = (
                    zed[p, near, here].astype(F32) + recv2[p, way, 0].astype(F32)
                ).astype(BF16)
            ring_start(phase, p, way, 2)

    def ring_end(phase, p):
        for way in range(2):
            for m in range(1, 3):
                ring_copy(phase, p, way, m).wait_recv()
        for half in range(2):
            low_m, high_m = (2, 1) if half == 0 else (1, 2)
            if phase == 0:
                for h in range(2):
                    total = dw[p, 0, half * 2 + h].astype(F32)
                    total += recv1[p, 0, low_m, h].astype(F32)
                    total += recv1[p, 1, high_m, h].astype(F32)
                    zed[p, half * 2 + h] = total.astype(BF16)
            else:
                here = pl.ds(half * 64, 64)
                total = zed[p, 0, here].astype(F32)
                total += recv2[p, 0, low_m].astype(F32)
                total += recv2[p, 1, high_m].astype(F32)
                target = gate_ref if p < pieces // 2 else up_ref
                q = p % (pieces // 2)
                target[here, q * tile : (q + 1) * tile] = total.astype(BF16)
        if phase == 0:
            ring_first(1, p)

    def combine():
        for part in range(2):
            for j in range(1, NJ):
                back_copy(part, j).wait_recv()
        for group in range(3, -1, -1):
            rows = pl.ds(group * 16, 16)
            for n in range(0, dim, 512):
                cols = slice(n, n + 512)
                parts = jnp.concatenate(
                    [rows_back[0, rows, cols]] + [returned[j, rows, cols] for j in range(1, NJ)], 0
                )
                sums = lax.dot_general(pm[group], parts, over_tokens, preferred_element_type=F32)
                yown[group * 4 : group * 4 + 4, :, cols] = sums.reshape(4, tok, 512)

    wide = dim // 2

    def line_copy(way, hop, half):
        return remote(
            zsend.at[way, hop - 1, half], zrecv.at[way, hop - 1, half],
            z_send.at[way, hop - 1, half], z_recv.at[way, hop - 1, half],
            z_dev(-1 if way == 0 else 1),
        )

    def line_start(way, hop, half):
        copy = line_copy(way, hop, half)
        copy.start()
        pending.append(copy)

    def line_far():
        for way in range(2):
            zsend[way, HALF - 1, way] = yown[15, :, way * wide : (way + 1) * wide].astype(BF16)
            line_start(way, HALF, way)

    def line_step(hop):
        halves = ((1, 0), (0, 1)) if hop == HALF - 1 else ((0, 1), (0, 1))
        for turn_ in range(2):
            for way in range(2):
                half = halves[way][turn_] if hop == HALF - 1 else turn_
                total = yown[slot_of(way, hop), :, half * wide : (half + 1) * wide]
                if hop < HALF - 1 or half == way:
                    line_copy(way, hop + 1, half).wait_recv()
                    total = total + zrecv[way, hop, half].astype(F32)
                zsend[way, hop - 1, half] = total.astype(BF16)
                line_start(way, hop, half)

    def line_end():
        for half in range(2):
            cols = slice(half * wide, (half + 1) * wide)
            total = yown[0, :, cols]
            for way in range(2):
                line_copy(way, 1, half).wait_recv()
                total = total + zrecv[way, 0, half].astype(F32)
            out_ref[:, cols] = total.astype(BF16)

    do = functools.partial
    tasks = []
    for p in range(pieces):
        weight_piece(p)
    x_pieces = [p for p in range(pieces) if order_of[p] == 0]
    ring_first(0, x_pieces[0])
    for p in range(pieces):
        if order_of[p] == 1:
            ring_first(0, p)
            tasks += [(10, do(ring_add, 0, p)), (26, do(ring_end, 0, p))]
            tasks += [(34, do(ring_add, 1, p)), (42, do(ring_end, 1, p))]
    back_start(0)
    row_grads(1)
    back_start(1)
    step = 8.6
    for i, p in enumerate(x_pieces):
        tasks.append((step * i + 5, do(ring_add, 0, p)))
        if i + 1 < len(x_pieces):
            tasks.append((step * i + 5.01, do(ring_first, 0, x_pieces[i + 1])))
        tasks.append((step * (i + 1) + 6, do(ring_end, 0, p)))
        tasks.append((step * (i + 1) + 12, do(ring_add, 1, p)))
        tasks.append((step * (i + 1) + 20, do(ring_end, 1, p)))
    tasks.append((11, combine))
    tasks.append((11.1, line_far))
    for hop in range(HALF - 1, 0, -1):
        tasks.append((11.2 + 5.3 * (HALF - hop), do(line_step, hop)))
    tasks.append((11.2 + 5.3 * HALF, line_end))
    for _, task in sorted(tasks, key=lambda entry: entry[0]):
        task()
    for copy in pending:
        copy.wait_send()


def hand_on(a, b, c, a_out, b_out, c_out):
    a_out[...] = a[...]
    b_out[...] = b[...]
    c_out[...] = c[...]


def body(quant_rows, row_scales, out_grads, routes, probs, w_gate, w_up, w_down):
    tok, dim = quant_rows.shape
    ff = w_gate.shape[2]
    pieces = 2 * ff // 256
    vmem = pl.BlockSpec(memory_space=pltpu.VMEM)
    hbm = pl.BlockSpec(memory_space=pl.ANY)
    dma = pltpu.SemaphoreType.DMA
    wide = dim // 2
    out, gate, up = pl.pallas_call(
        kernel,
        out_shape=(
            jax.ShapeDtypeStruct((tok, dim), BF16),
            jax.ShapeDtypeStruct((128, ff), BF16),
            jax.ShapeDtypeStruct((128, ff), BF16),
        ),
        in_specs=[vmem] * 5 + [hbm] * 3,
        out_specs=(vmem, vmem, vmem),
        scratch_shapes=[
            pltpu.VMEM((dim, ff), BF16),
            pltpu.VMEM((dim, ff), BF16),
            pltpu.VMEM((ff, dim), BF16),
            pltpu.VMEM((NZ, 8, NJ * tok), F32),
            pltpu.VMEM((NZ, tok, dim), BF16),
            pltpu.VMEM((NZ, tok, dim), BF16),
            pltpu.VMEM((4, 64, NJ * tok), BF16),
            pltpu.VMEM((2, 4, NJ, 16, dim), BF16),
            pltpu.VMEM((2, 4, NJ, 16, dim), BF16),
            pltpu.VMEM((dim // 256, 256, 256), BF16),
            pltpu.VMEM((pieces, 256, 256), BF16),
            pltpu.VMEM((NJ, 64, dim), BF16),
            pltpu.VMEM((NJ, 64, dim), BF16),
            pltpu.VMEM((NZ, tok, dim), F32),
            pltpu.VMEM((2, HALF, 2, tok, wide), BF16),
            pltpu.VMEM((2, HALF, 2, tok, wide), BF16),
            pltpu.VMEM((pieces, 4, 4, 128, 256), BF16),
            pltpu.VMEM((pieces, 4, 128, 256), BF16),
            pltpu.VMEM((pieces, 2, 3, 2, 128, 256), BF16),
            pltpu.VMEM((pieces, 2, 3, 64, 256), BF16),
            dma((3,)),
            dma((2, HALF, SUBS)),
            dma((2, HALF, SUBS)),
            dma((4, 3, 2)),
            dma((4, 3, 2)),
            dma((2, 3)),
            dma((2, 3)),
            dma((2, HALF, 2)),
            dma((2, HALF, 2)),
            dma((2, pieces, 2, 3)),
            dma((2, pieces, 2, 3)),
        ],
        compiler_params=pltpu.CompilerParams(
            collective_id=0, has_side_effects=True, vmem_limit_bytes=60 * 1024 * 1024
        ),
    )(
        quant_rows, row_scales.reshape(1, tok), out_grads, routes.T, probs.T,
        w_gate[0], w_up[0], w_down[0],
    )
    out, gate, up = pl.pallas_call(
        hand_on,
        out_shape=tuple(jax.ShapeDtypeStruct(a.shape, a.dtype) for a in (out, gate, up)),
        in_specs=[vmem] * 3,
        out_specs=(vmem,) * 3,
    )(out, gate, up)
    return out, gate[None], up[None]


def solution(mesh):
    in_specs = (
        P(("rep", "exp"), None),
        P(("rep", "exp")),
        P(("rep", "exp"), None),
        P(("rep", "exp"), None),
        P(("rep", "exp"), None),
        P("exp", None, None),
        P("exp", None, None),
        P("exp", None, None),
    )
    out_specs = (P(("rep", "exp"), None), P("exp", "rep", None), P("exp", "rep", None))
    return jax.shard_map(body, mesh=mesh, in_specs=in_specs, out_specs=out_specs, check_vma=False)
```

```python
import functools

import jax
import jax.numpy as jnp
from jax import lax
from jax.experimental import pallas as pl
from jax.experimental.pallas import tpu as pltpu
from jax.sharding import PartitionSpec as P

MESH = pl.DeviceIdType.MESH
F32 = jnp.float32
BF16 = jnp.bfloat16

NX, NYH, NZ, NC = 4, 4, 16, 2
NJ = 4
HALF = NZ // 2
CAP = 4
SUBS = 3


def kernel(
    x_ref, scale_ref, g_ref, routes_ref, probs_ref, wg_hbm, wu_hbm, wd_hbm,
    out_ref, gate_ref, up_ref,
    wg, wu, wd, meta, xs, gs, pm, stage, got, xt, both, rows_back, returned, yown,
    zsend, zrecv, dw, zed, recv1, recv2,
    w_sem, f_send, f_recv, p_send, p_recv, b_send, b_recv, z_send, z_recv, r_send, r_recv,
):
    tok, dim = x_ref.shape
    ff = wg.shape[1]
    tile = 256
    pieces = 2 * ff // tile
    rep, exp = lax.axis_index("rep"), lax.axis_index("exp")
    my_x, my_y = rep // NYH, rep % NYH
    y_lo, z, core = exp // (NZ * NC), exp // NC % NZ, exp % NC

    def z_dev(step):
        return (rep, y_lo * (NZ * NC) + (z + NZ + step) % NZ * NC + core)

    def plane_exp(j):
        other_y = 1 - y_lo if j // 2 else y_lo
        other_c = 1 - core if j % 2 else core
        return other_y * (NZ * NC) + z * NC + other_c

    def x_dev(step):
        return ((my_x + NX + step) % NX * NYH + my_y, exp)

    def y_dev(step):
        return (my_x * NYH + (my_y + NYH + step) % NYH, exp)

    weights = [
        pltpu.make_async_copy(src, dst, w_sem.at[i])
        for i, (src, dst) in enumerate(((wg_hbm, wg), (wu_hbm, wu), (wd_hbm, wd)))
    ]
    for copy in weights:
        copy.start()

    neighbours = [z_dev(1), z_dev(-1), x_dev(1), x_dev(-1), y_dev(1), y_dev(-1)]
    neighbours += [(rep, plane_exp(j)) for j in range(1, NJ)]
    barrier = pltpu.get_barrier_semaphore()
    for device in neighbours:
        pl.semaphore_signal(barrier, inc=1, device_id=device, device_id_type=MESH)

    def iota(shape, axis):
        return lax.broadcasted_iota(jnp.int32, shape, axis)

    diag = jnp.where(iota((tok, tok), 0) == iota((tok, tok), 1), scale_ref[...].astype(F32), 0.0)
    diag = diag.astype(BF16)
    xs[0] = jnp.dot(diag, x_ref[...], preferred_element_type=F32).astype(BF16)
    gs[0] = g_ref[...]
    lanes = NJ * tok
    spread = (iota((tok, lanes), 1) % tok == iota((tok, lanes), 0)).astype(BF16)
    over_tokens = (((0,), (0,)), ((), ()))
    table = jnp.dot(
        routes_ref[...].astype(F32).astype(BF16), spread, preferred_element_type=F32
    )
    chance = jnp.dot(probs_ref[...], spread, preferred_element_type=F32)
    experts = NJ * NZ
    hits = [iota((experts, lanes), 0).astype(F32) == table[k : k + 1] for k in range(4)]
    named = sum(hit.astype(F32) for hit in hits)
    a, b = iota((lanes, lanes), 0), iota((lanes, lanes), 1)
    before = ((a // tok == b // tok) & (a < b)).astype(BF16)
    rank = jnp.dot(named.astype(BF16), before, preferred_element_type=F32)
    for k in range(4):
        mine = jnp.sum(jnp.where(hits[k], rank, 0.0), axis=0, keepdims=True)
        meta[0, k : k + 1, :] = table[k : k + 1] * CAP + mine
        meta[0, 4 + k : 5 + k, :] = chance[k : k + 1]

    pl.semaphore_wait(barrier, len(neighbours))

    pending = []

    def remote(src, dst, send, recv, device):
        return pltpu.make_async_remote_copy(
            src_ref=src, dst_ref=dst, send_sem=send, recv_sem=recv,
            device_id=device, device_id_type=MESH,
        )

    travels = (meta, xs, gs)

    def slot_of(way, hop):
        return 0 if hop == 0 else 15 if hop == HALF else 2 * hop - 1 + way

    def carries(way, hop, sub):
        return hop < HALF or (sub == 2) == (way == 1)

    def hop_copy(way, hop, sub):
        buf = travels[sub]
        return remote(
            buf.at[slot_of(way, hop - 1)], buf.at[slot_of(way, hop)],
            f_send.at[way, hop - 1, sub], f_recv.at[way, hop - 1, sub],
            z_dev(1 if way == 0 else -1),
        )

    def hop_start(way, hop, sub):
        if hop <= HALF and carries(way, hop, sub):
            copy = hop_copy(way, hop, sub)
            copy.start()
            pending.append(copy)

    for sub in range(SUBS):
        for way in range(2):
            hop_start(way, 1, sub)

    group_rows = NJ * 4 * CAP
    r = iota((group_rows, lanes), 0)
    c = iota((group_rows, lanes), 1)
    expert_of = jnp.where(
        r // 16 == 0, plane_exp(0),
        jnp.where(r // 16 == 1, plane_exp(1), jnp.where(r // 16 == 2, plane_exp(2), plane_exp(3))),
    )
    slot_id = jnp.where(r % 16 // CAP == c // tok, expert_of * CAP + r % CAP, -1).astype(F32)

    def plane_copy(group, j, kind):
        return remote(
            stage.at[kind, group, j], got.at[kind, group, j],
            p_send.at[group, j - 1, kind], p_recv.at[group, j - 1, kind], (rep, plane_exp(j)),
        )

    def select(group):
        lane_group = iota((8, lanes), 1) // tok
        mix = meta[group * 4]
        for m in range(1, 4):
            mix = jnp.where(lane_group == m, meta[group * 4 + m], mix)
        hit = [slot_id == mix[k : k + 1] for k in range(4)]
        ones = sum(h.astype(F32) for h in hit)
        pm[group] = ones.astype(BF16)
        weighed = sum(jnp.where(hit[k], mix[4 + k : 5 + k], 0.0) for k in range(4))
        picks = (pm[group], weighed.astype(BF16))
        for kind, buf in ((0, xs), (1, gs)):
            for n in range(0, dim, 512):
                block = buf[group * 4 : group * 4 + 4, :, n : n + 512].reshape(4 * tok, 512)
                chosen = jnp.dot(picks[kind], block, preferred_element_type=F32).astype(BF16)
                got[kind, group, 0, :, n : n + 512] = chosen[:16]
                stage[kind, group, 1:, :, n : n + 512] = chosen[16:].reshape(3, 16, 512)
            for j in range(1, NJ):
                copy = plane_copy(group, j, kind)
                copy.start()
                pending.append(copy)

    slots = NJ * 64
    over_last = (((1,), (1,)), ((), ()))

    def project(low, high, arrived=None, ready=None):
        for group in range(low, high):
            for j in range(1, NJ):
                for kind in range(2):
                    plane_copy(group, j, kind).wait_recv()
        if arrived is not None:
            arrived()
        here, count = slice(low * 64, high * 64), (high - low) * 64
        for n in range(dim // tile):
            block = got[0, low:high, :, :, n * tile : (n + 1) * tile]
            xt[n, :, here] = block.reshape(count, tile).T
        for f in range(ff // tile):
            cols = slice(f * tile, (f + 1) * tile)
            ins = got[0, low:high].reshape(count, dim)
            gate = jnp.dot(ins, wg[:, cols], preferred_element_type=F32)
            up = jnp.dot(ins, wu[:, cols], preferred_element_type=F32)
            grads = got[1, low:high].reshape(count, dim)
            hidden = lax.dot_general(grads, wd[cols, :], over_last, preferred_element_type=F32)
            s = jax.nn.sigmoid(gate)
            both[f, here] = (hidden * up * s * (1.0 + gate * (1.0 - s))).astype(BF16)
            both[f + ff // tile, here] = (hidden * gate * s).astype(BF16)
            if ready is not None:
                ready(f)

    def back_copy(part, j):
        rows = pl.ds(0, 48) if part == 0 else pl.ds(48, 16)
        return remote(
            rows_back.at[j, rows], returned.at[j, rows],
            b_send.at[part, j - 1], b_recv.at[part, j - 1], (rep, plane_exp(j)),
        )

    def row_grads(part):
        low, high = ((0, 3), (3, 4))[part]
        here, count = slice(low * 64, high * 64), (high - low) * 64

        def one(n, carry):
            cols = pl.ds(pl.multiple_of(n * tile, tile), tile)
            total = jnp.zeros((count, tile), F32)
            for k in range(ff // tile):
                inner = slice(k * tile, (k + 1) * tile)
                total += lax.dot_general(
                    both[k, here], wg[cols, inner], over_last, preferred_element_type=F32
                )
                total += lax.dot_general(
                    both[k + ff // tile, here], wu[cols, inner], over_last,
                    preferred_element_type=F32,
                )
            value = total.astype(BF16).reshape(high - low, NJ, 16, tile)
            for j in range(NJ):
                rows = slice(low * 16, high * 16)
                rows_back[j, rows, cols] = value[:, j].reshape(count // NJ, tile)
            return carry

        lax.fori_loop(0, dim // tile, one, 0)

    def back_start(part):
        for j in range(1, NJ):
            copy = back_copy(part, j)
            copy.start()
            pending.append(copy)

    for hop in range(1, HALF + 1):
        for sub in range(SUBS):
            for way in range(2):
                if carries(way, hop, sub):
                    hop_copy(way, hop, sub).wait_recv()
                    hop_start(way, hop + 1, sub)
        if hop == 2:
            for copy in weights:
                copy.wait()
        if hop % 2 == 0:
            select(hop // 2 - 1)
        elif hop == 5:
            project(0, 2)
    project(2, 3)
    row_grads(0)

    axes = ((x_dev, y_dev), (y_dev, x_dev))
    thirds = ff // tile
    order_of = [1 if p == thirds else 0 for p in range(pieces)]

    def weight_piece(p):
        order = order_of[p]

        for i in range(dim // tile):
            value = jnp.dot(xt[i], both[p], preferred_element_type=F32).astype(BF16)
            rx = (i // 2 - my_x + NX) % NX
            for h in range(2):
                ry = (2 * (i % 2) + h - my_y + NYH) % NYH
                part = value[h * 128 : (h + 1) * 128]
                if order == 0:
                    dw[p, rx, ry] = part
                else:
                    dw[p, ry, rx] = part

    def ring_copy(phase, p, way, m):
        to = axes[order_of[p]][phase](1 if way == 0 else -1)
        near = 1 if way == 0 else 3
        block = (2, near, near)[m]
        half = (way, 1 - way, way)[m]
        if phase == 0:
            src = dw.at[p, block, pl.ds(half * 2, 2)]
            dst = recv1.at[p, way, m]
        else:
            src = zed.at[p, block, pl.ds(half * 64, 64)]
            dst = recv2.at[p, way, m]
        return remote(src, dst, r_send.at[phase, p, way, m], r_recv.at[phase, p, way, m], to)

    def ring_start(phase, p, way, m):
        copy = ring_copy(phase, p, way, m)
        copy.start()
        pending.append(copy)

    def ring_send(phase, p, m):
        for way in range(2):
            ring_start(phase, p, way, m)

    def ring_first(phase, p):
        for m in range(2):
            ring_send(phase, p, m)

    def ring_add(phase, p):
        for way in range(2):
            ring_copy(phase, p, way, 0).wait_recv()
            near = 1 if way == 0 else 3
            if phase == 0:
                for h in range(2):
                    dw[p, near, way * 2 + h] = (
                        dw[p, near, way * 2 + h].astype(F32) + recv1[p, way, 0, h].astype(F32)
                    ).astype(BF16)
            else:
                here = pl.ds(way * 64, 64)
                zed[p, near, here] = (
                    zed[p, near, here].astype(F32) + recv2[p, way, 0].astype(F32)
                ).astype(BF16)
            ring_start(phase, p, way, 2)

    def ring_end(phase, p):
        for way in range(2):
            for m in range(1, 3):
                ring_copy(phase, p, way, m).wait_recv()
        for half in range(2):
            low_m, high_m = (2, 1) if half == 0 else (1, 2)
            if phase == 0:
                for h in range(2):
                    total = dw[p, 0, half * 2 + h].astype(F32)
                    total += recv1[p, 0, low_m, h].astype(F32)
                    total += recv1[p, 1, high_m, h].astype(F32)
                    zed[p, half * 2 + h] = total.astype(BF16)
            else:
                here = pl.ds(half * 64, 64)
                total = zed[p, 0, here].astype(F32)
                total += recv2[p, 0, low_m].astype(F32)
                total += recv2[p, 1, high_m].astype(F32)
                target = gate_ref if p < pieces // 2 else up_ref
                q = p % (pieces // 2)
                target[here, q * tile : (q + 1) * tile] = total.astype(BF16)
        if phase == 0:
            ring_first(1, p)

    def combine():
        for part in range(2):
            for j in range(1, NJ):
                back_copy(part, j).wait_recv()
        for group in range(3, -1, -1):
            rows = pl.ds(group * 16, 16)
            for n in range(0, dim, 512):
                cols = slice(n, n + 512)
                parts = jnp.concatenate(
                    [rows_back[0, rows, cols]] + [returned[j, rows, cols] for j in range(1, NJ)], 0
                )
                sums = lax.dot_general(pm[group], parts, over_tokens, preferred_element_type=F32)
                yown[group * 4 : group * 4 + 4, :, cols] = sums.reshape(4, tok, 512)

    wide = dim // 2

    def line_copy(way, hop, half):
        return remote(
            zsend.at[way, hop - 1, half], zrecv.at[way, hop - 1, half],
            z_send.at[way, hop - 1, half], z_recv.at[way, hop - 1, half],
            z_dev(-1 if way == 0 else 1),
        )

    def line_start(way, hop, half):
        copy = line_copy(way, hop, half)
        copy.start()
        pending.append(copy)

    def line_far():
        for way in range(2):
            zsend[way, HALF - 1, way] = yown[15, :, way * wide : (way + 1) * wide].astype(BF16)
            line_start(way, HALF, way)

    def line_step(hop):
        halves = ((1, 0), (0, 1)) if hop == HALF - 1 else ((0, 1), (0, 1))
        for turn_ in range(2):
            for way in range(2):
                half = halves[way][turn_] if hop == HALF - 1 else turn_
                total = yown[slot_of(way, hop), :, half * wide : (half + 1) * wide]
                if hop < HALF - 1 or half == way:
                    line_copy(way, hop + 1, half).wait_recv()
                    total = total + zrecv[way, hop, half].astype(F32)
                zsend[way, hop - 1, half] = total.astype(BF16)
                line_start(way, hop, half)

    def line_end():
        for half in range(2):
            cols = slice(half * wide, (half + 1) * wide)
            total = yown[0, :, cols]
            for way in range(2):
                line_copy(way, 1, half).wait_recv()
                total = total + zrecv[way, 0, half].astype(F32)
            out_ref[:, cols] = total.astype(BF16)

    do = functools.partial
    y_piece = thirds
    x_pieces = [p + half * thirds for p in range(thirds) for half in range(2)]
    x_pieces.remove(y_piece)

    def ready(f):
        weight_piece(f)
        if f == 0:
            ring_first(0, x_pieces[0])
        elif f == 1:
            ring_send(0, x_pieces[1], 0)
        weight_piece(f + thirds)

    project(3, 4, do(back_start, 0), ready)
    row_grads(1)
    back_start(1)
    ring_first(0, y_piece)
    step = 8.6
    tasks = [(26, do(ring_add, 0, y_piece)), (42, do(ring_end, 0, y_piece))]
    tasks += [(48, do(ring_add, 1, y_piece)), (54, do(ring_end, 1, y_piece))]
    for i, p in enumerate(x_pieces):
        when = step * i + 5
        tasks.append((when, do(ring_add, 0, p)))
        if i + 1 < len(x_pieces):
            tasks.append((when + 0.01, do(ring_send, 0, x_pieces[i + 1], 1)))
        if i + 2 < len(x_pieces):
            tasks.append((when + 0.02, do(ring_send, 0, x_pieces[i + 2], 0)))
        tasks.append((when + 9.6, do(ring_end, 0, p)))
        tasks.append((when + 15.6, do(ring_add, 1, p)))
        tasks.append((when + 23.6, do(ring_end, 1, p)))
    tasks.append((16, combine))
    tasks.append((16.1, line_far))
    for hop in range(HALF - 1, 0, -1):
        tasks.append((16.2 + 4.6 * (HALF - hop), do(line_step, hop)))
    tasks.append((16.2 + 4.6 * HALF, line_end))
    for _, task in sorted(tasks, key=lambda entry: entry[0]):
        task()
    for copy in pending:
        copy.wait_send()


def hand_on(a, b, c, a_out, b_out, c_out):
    a_out[...] = a[...]
    b_out[...] = b[...]
    c_out[...] = c[...]


def body(quant_rows, row_scales, out_grads, routes, probs, w_gate, w_up, w_down):
    tok, dim = quant_rows.shape
    ff = w_gate.shape[2]
    pieces = 2 * ff // 256
    vmem = pl.BlockSpec(memory_space=pltpu.VMEM)
    hbm = pl.BlockSpec(memory_space=pl.ANY)
    dma = pltpu.SemaphoreType.DMA
    wide = dim // 2
    out, gate, up = pl.pallas_call(
        kernel,
        out_shape=(
            jax.ShapeDtypeStruct((tok, dim), BF16),
            jax.ShapeDtypeStruct((128, ff), BF16),
            jax.ShapeDtypeStruct((128, ff), BF16),
        ),
        in_specs=[vmem] * 5 + [hbm] * 3,
        out_specs=(vmem, vmem, vmem),
        scratch_shapes=[
            pltpu.VMEM((dim, ff), BF16),
            pltpu.VMEM((dim, ff), BF16),
            pltpu.VMEM((ff, dim), BF16),
            pltpu.VMEM((NZ, 8, NJ * tok), F32),
            pltpu.VMEM((NZ, tok, dim), BF16),
            pltpu.VMEM((NZ, tok, dim), BF16),
            pltpu.VMEM((4, 64, NJ * tok), BF16),
            pltpu.VMEM((2, 4, NJ, 16, dim), BF16),
            pltpu.VMEM((2, 4, NJ, 16, dim), BF16),
            pltpu.VMEM((dim // 256, 256, 256), BF16),
            pltpu.VMEM((pieces, 256, 256), BF16),
            pltpu.VMEM((NJ, 64, dim), BF16),
            pltpu.VMEM((NJ, 64, dim), BF16),
            pltpu.VMEM((NZ, tok, dim), F32),
            pltpu.VMEM((2, HALF, 2, tok, wide), BF16),
            pltpu.VMEM((2, HALF, 2, tok, wide), BF16),
            pltpu.VMEM((pieces, 4, 4, 128, 256), BF16),
            pltpu.VMEM((pieces, 4, 128, 256), BF16),
            pltpu.VMEM((pieces, 2, 3, 2, 128, 256), BF16),
            pltpu.VMEM((pieces, 2, 3, 64, 256), BF16),
            dma((3,)),
            dma((2, HALF, SUBS)),
            dma((2, HALF, SUBS)),
            dma((4, 3, 2)),
            dma((4, 3, 2)),
            dma((2, 3)),
            dma((2, 3)),
            dma((2, HALF, 2)),
            dma((2, HALF, 2)),
            dma((2, pieces, 2, 3)),
            dma((2, pieces, 2, 3)),
        ],
        compiler_params=pltpu.CompilerParams(
            collective_id=0, has_side_effects=True, vmem_limit_bytes=60 * 1024 * 1024
        ),
    )(
        quant_rows, row_scales.reshape(1, tok), out_grads, routes.T, probs.T,
        w_gate[0], w_up[0], w_down[0],
    )
    out, gate, up = pl.pallas_call(
        hand_on,
        out_shape=tuple(jax.ShapeDtypeStruct(a.shape, a.dtype) for a in (out, gate, up)),
        in_specs=[vmem] * 3,
        out_specs=(vmem,) * 3,
    )(out, gate, up)
    return out, gate[None], up[None]


def solution(mesh):
    in_specs = (
        P(("rep", "exp"), None),
        P(("rep", "exp")),
        P(("rep", "exp"), None),
        P(("rep", "exp"), None),
        P(("rep", "exp"), None),
        P("exp", None, None),
        P("exp", None, None),
        P("exp", None, None),
    )
    out_specs = (P(("rep", "exp"), None), P("exp", "rep", None), P("exp", "rep", None))
    return jax.shard_map(body, mesh=mesh, in_specs=in_specs, out_specs=out_specs, check_vma=False)
```

```python
import functools

import jax
import jax.numpy as jnp
from jax import lax
from jax.experimental import pallas as pl
from jax.experimental.pallas import tpu as pltpu
from jax.sharding import PartitionSpec as P

MESH = pl.DeviceIdType.MESH
F32 = jnp.float32
BF16 = jnp.bfloat16

NX, NYH, NZ, NC = 4, 4, 16, 2
NJ = 4
HALF = NZ // 2
CAP = 4
SUBS = 3


def kernel(
    x_ref, scale_ref, g_ref, routes_ref, probs_ref, wg_hbm, wu_hbm, wd_hbm,
    out_ref, gate_ref, up_ref,
    wg, wu, wd, meta, xs, gs, pm, stage, got, xt, both, rows_back, returned, yown,
    zsend, zrecv, dw, zed, recv1, recv2, far_send, far_recv,
    w_sem, f_send, f_recv, p_send, p_recv, b_send, b_recv, z_send, z_recv, r_send, r_recv,
    q_send, q_recv,
):
    tok, dim = x_ref.shape
    ff = wg.shape[1]
    tile = 256
    pieces = 2 * ff // tile
    rep, exp = lax.axis_index("rep"), lax.axis_index("exp")
    my_x, my_y = rep // NYH, rep % NYH
    y_lo, z, core = exp // (NZ * NC), exp // NC % NZ, exp % NC

    def z_dev(step):
        return (rep, y_lo * (NZ * NC) + (z + NZ + step) % NZ * NC + core)

    def plane_exp(j):
        other_y = 1 - y_lo if j // 2 else y_lo
        other_c = 1 - core if j % 2 else core
        return other_y * (NZ * NC) + z * NC + other_c

    def x_dev(step):
        return ((my_x + NX + step) % NX * NYH + my_y, exp)

    def y_dev(step):
        return (my_x * NYH + (my_y + NYH + step) % NYH, exp)

    weights = [
        pltpu.make_async_copy(src, dst, w_sem.at[i])
        for i, (src, dst) in enumerate(((wg_hbm, wg), (wu_hbm, wu), (wd_hbm, wd)))
    ]
    for copy in weights:
        copy.start()

    neighbours = [z_dev(1), z_dev(-1), x_dev(1), x_dev(-1), y_dev(1), y_dev(-1)]
    neighbours += [(rep, plane_exp(j)) for j in range(1, NJ)]
    barrier = pltpu.get_barrier_semaphore()
    for device in neighbours:
        pl.semaphore_signal(barrier, inc=1, device_id=device, device_id_type=MESH)

    def iota(shape, axis):
        return lax.broadcasted_iota(jnp.int32, shape, axis)

    diag = jnp.where(iota((tok, tok), 0) == iota((tok, tok), 1), scale_ref[...].astype(F32), 0.0)
    diag = diag.astype(BF16)
    xs[12] = jnp.dot(diag, x_ref[...], preferred_element_type=F32).astype(BF16)
    gs[12] = g_ref[...]
    lanes = NJ * tok
    spread = (iota((tok, lanes), 1) % tok == iota((tok, lanes), 0)).astype(BF16)
    over_tokens = (((0,), (0,)), ((), ()))
    table = jnp.dot(
        routes_ref[...].astype(F32).astype(BF16), spread, preferred_element_type=F32
    )
    chance = jnp.dot(probs_ref[...], spread, preferred_element_type=F32)
    experts = NJ * NZ
    hits = [iota((experts, lanes), 0).astype(F32) == table[k : k + 1] for k in range(4)]
    named = sum(hit.astype(F32) for hit in hits)
    a, b = iota((lanes, lanes), 0), iota((lanes, lanes), 1)
    before = ((a // tok == b // tok) & (a < b)).astype(BF16)
    rank = jnp.dot(named.astype(BF16), before, preferred_element_type=F32)
    for k in range(4):
        mine = jnp.sum(jnp.where(hits[k], rank, 0.0), axis=0, keepdims=True)
        meta[12, k : k + 1, :] = table[k : k + 1] * CAP + mine
        meta[12, 4 + k : 5 + k, :] = chance[k : k + 1]

    pl.semaphore_wait(barrier, len(neighbours))

    pending = []

    def remote(src, dst, send, recv, device):
        return pltpu.make_async_remote_copy(
            src_ref=src, dst_ref=dst, send_sem=send, recv_sem=recv,
            device_id=device, device_id_type=MESH,
        )

    travels = (meta, xs, gs)

    def slot_of(way, hop):
        near = {0: 12, 1: 13 + way, HALF: 15}
        return near[hop] if hop in near else 2 * (hop - 2) + way

    def carries(way, hop, sub):
        return hop < HALF or (sub == 2) == (way == 1)

    def hop_copy(way, hop, sub):
        buf = travels[sub]
        return remote(
            buf.at[slot_of(way, hop - 1)], buf.at[slot_of(way, hop)],
            f_send.at[way, hop - 1, sub], f_recv.at[way, hop - 1, sub],
            z_dev(1 if way == 0 else -1),
        )

    def hop_start(way, hop, sub):
        if hop <= HALF and carries(way, hop, sub):
            copy = hop_copy(way, hop, sub)
            copy.start()
            pending.append(copy)

    for sub in range(SUBS):
        for way in range(2):
            hop_start(way, 1, sub)

    group_rows = NJ * 4 * CAP
    r = iota((group_rows, lanes), 0)
    c = iota((group_rows, lanes), 1)
    expert_of = jnp.where(
        r // 16 == 0, plane_exp(0),
        jnp.where(r // 16 == 1, plane_exp(1), jnp.where(r // 16 == 2, plane_exp(2), plane_exp(3))),
    )
    slot_id = jnp.where(r % 16 // CAP == c // tok, expert_of * CAP + r % CAP, -1).astype(F32)

    def plane_copy(group, j, kind):
        return remote(
            stage.at[kind, group, j], got.at[kind, group, j],
            p_send.at[group, j - 1, kind], p_recv.at[group, j - 1, kind], (rep, plane_exp(j)),
        )

    def picks(group):
        lane_group = iota((8, lanes), 1) // tok
        mix = meta[group * 4]
        for m in range(1, 4):
            mix = jnp.where(lane_group == m, meta[group * 4 + m], mix)
        hit = [slot_id == mix[k : k + 1] for k in range(4)]
        ones = sum(h.astype(F32) for h in hit)
        weighed = sum(jnp.where(hit[k], mix[4 + k : 5 + k], 0.0) for k in range(4))
        return ones.astype(BF16), weighed.astype(BF16)

    def select(group, kind):
        members = 4 if group < 3 else 3
        pick = picks(group)
        if kind == 0:
            pm[group] = pick[0]
        chosen_of = pick[kind][:, : members * tok]
        buf = travels[1 + kind]
        for n in range(0, dim, 512):
            block = buf[group * 4 : group * 4 + members, :, n : n + 512]
            block = block.reshape(members * tok, 512)
            chosen = jnp.dot(chosen_of, block, preferred_element_type=F32).astype(BF16)
            got[kind, group, 0, :, n : n + 512] = chosen[:16]
            stage[kind, group, 1:, :, n : n + 512] = chosen[16:].reshape(3, 16, 512)
        for j in range(1, NJ):
            copy = plane_copy(group, j, kind)
            copy.start()
            pending.append(copy)

    quarter = dim // 4

    def far_copy(j, kind):
        return remote(
            far_send.at[kind, j - 1], far_recv.at[kind, j - 1],
            q_send.at[j - 1, kind], q_recv.at[j - 1, kind], (rep, plane_exp(j)),
        )

    def far_picks(slot):
        last = meta[15][:, :tok]
        hit = [slot == last[k : k + 1] for k in range(4)]
        ones = sum(h.astype(F32) for h in hit)
        weighed = sum(jnp.where(hit[k], last[4 + k : 5 + k], 0.0) for k in range(4))
        return ones, weighed

    def select_far():
        pm[3] = picks(3)[0]
        row = iota((48, tok), 0)
        owner = jnp.where(
            row // 16 == 0, plane_exp(1), jnp.where(row // 16 == 1, plane_exp(2), plane_exp(3))
        )
        sent = far_picks((owner * CAP + row % CAP).astype(F32))
        for kind in range(2):
            buf = travels[1 + kind]
            total = jnp.zeros((48, quarter), F32)
            for q in range(4):
                pick = jnp.where(row % 16 // CAP == q, sent[kind], 0.0).astype(BF16)
                block = buf[15, :, q * quarter : (q + 1) * quarter]
                total += jnp.dot(pick, block, preferred_element_type=F32)
            far_send[kind] = total.astype(BF16).reshape(3, 16, quarter)
            for j in range(1, NJ):
                copy = far_copy(j, kind)
                copy.start()
                pending.append(copy)
        row = iota((16, tok), 0)
        slot = jnp.where(row // CAP == 3, plane_exp(0) * CAP + row % CAP, -1)
        kept = far_picks(slot.astype(F32))
        for kind in range(2):
            buf = travels[1 + kind]
            for n in range(0, dim, 512):
                cols = slice(n, n + 512)
                more = jnp.dot(
                    kept[kind].astype(BF16), buf[15, :, cols], preferred_element_type=F32
                )
                got[kind, 3, 0, :, cols] = (got[kind, 3, 0, :, cols].astype(F32) + more).astype(BF16)

    def unpack_far():
        a, b = iota((48, 48), 0), iota((48, 48), 1)
        same = (a // 16 == b // 16) & (a % 16 // CAP == 3) & (a % CAP == b % CAP)
        for kind in range(2):
            for j in range(1, NJ):
                far_copy(j, kind).wait_recv()
            packed = far_recv[kind].reshape(48, quarter)
            for q in range(4):
                cols = slice(q * quarter, (q + 1) * quarter)
                place = (same & (b % 16 // CAP == q)).astype(F32).astype(BF16)
                more = jnp.dot(place, packed, preferred_element_type=F32)
                old = got[kind, 3, 1:, :, cols].reshape(48, quarter).astype(F32)
                got[kind, 3, 1:, :, cols] = (old + more).astype(BF16).reshape(3, 16, quarter)

    slots = NJ * 64
    over_last = (((1,), (1,)), ((), ()))

    def project(low, high, arrived=None, ready=None):
        for group in range(low, high):
            for j in range(1, NJ):
                for kind in range(2):
                    plane_copy(group, j, kind).wait_recv()
        if arrived is not None:
            arrived()
        here, count = slice(low * 64, high * 64), (high - low) * 64
        for n in range(dim // tile):
            block = got[0, low:high, :, :, n * tile : (n + 1) * tile]
            xt[n, :, here] = block.reshape(count, tile).T
        for f in range(ff // tile):
            cols = slice(f * tile, (f + 1) * tile)
            ins = got[0, low:high].reshape(count, dim)
            gate = jnp.dot(ins, wg[:, cols], preferred_element_type=F32)
            up = jnp.dot(ins, wu[:, cols], preferred_element_type=F32)
            grads = got[1, low:high].reshape(count, dim)
            hidden = lax.dot_general(grads, wd[cols, :], over_last, preferred_element_type=F32)
            s = jax.nn.sigmoid(gate)
            both[f, here] = (hidden * up * s * (1.0 + gate * (1.0 - s))).astype(BF16)
            both[f + ff // tile, here] = (hidden * gate * s).astype(BF16)
            if ready is not None:
                ready(f)

    def back_copy(part, j):
        rows = pl.ds(part * 32, 32)
        return remote(
            rows_back.at[j, rows], returned.at[j, rows],
            b_send.at[part, j - 1], b_recv.at[part, j - 1], (rep, plane_exp(j)),
        )

    def row_grads(part):
        low, high = ((0, 2), (2, 4))[part]
        here, count = slice(low * 64, high * 64), (high - low) * 64

        def one(n, carry):
            cols = pl.ds(pl.multiple_of(n * tile, tile), tile)
            total = jnp.zeros((count, tile), F32)
            for k in range(ff // tile):
                inner = slice(k * tile, (k + 1) * tile)
                total += lax.dot_general(
                    both[k, here], wg[cols, inner], over_last, preferred_element_type=F32
                )
                total += lax.dot_general(
                    both[k + ff // tile, here], wu[cols, inner], over_last,
                    preferred_element_type=F32,
                )
            value = total.astype(BF16).reshape(high - low, NJ, 16, tile)
            for j in range(NJ):
                rows = slice(low * 16, high * 16)
                rows_back[j, rows, cols] = value[:, j].reshape(count // NJ, tile)
            return carry

        lax.fori_loop(0, dim // tile, one, 0)

    def back_start(part):
        for j in range(1, NJ):
            copy = back_copy(part, j)
            copy.start()
            pending.append(copy)

    group_at = {1: 3, 3: 0, 5: 1, 7: 2}
    for hop in range(1, HALF + 1):
        for sub in range(SUBS):
            for way in range(2):
                if carries(way, hop, sub):
                    hop_copy(way, hop, sub).wait_recv()
                    hop_start(way, hop + 1, sub)
            if hop in group_at and sub > 0:
                select(group_at[hop], sub - 1)
        if hop == 2:
            for copy in weights:
                copy.wait()
        if hop >= 6 and hop < HALF:
            project(hop - 6, hop - 5)
    select_far()
    row_grads(0)

    axes = ((x_dev, y_dev), (y_dev, x_dev))
    thirds = ff // tile
    order_of = [1 if p == thirds else 0 for p in range(pieces)]

    def weight_piece(p):
        order = order_of[p]

        for i in range(dim // tile):
            value = jnp.dot(xt[i], both[p], preferred_element_type=F32).astype(BF16)
            rx = (i // 2 - my_x + NX) % NX
            for h in range(2):
                ry = (2 * (i % 2) + h - my_y + NYH) % NYH
                part = value[h * 128 : (h + 1) * 128]
                if order == 0:
                    dw[p, rx, ry] = part
                else:
                    dw[p, ry, rx] = part

    def ring_copy(phase, p, way, m):
        to = axes[order_of[p]][phase](1 if way == 0 else -1)
        near = 1 if way == 0 else 3
        block = (2, near, near)[m]
        half = (way, 1 - way, way)[m]
        if phase == 0:
            src = dw.at[p, block, pl.ds(half * 2, 2)]
            dst = recv1.at[p, way, m]
        else:
            src = zed.at[p, block, pl.ds(half * 64, 64)]
            dst = recv2.at[p, way, m]
        return remote(src, dst, r_send.at[phase, p, way, m], r_recv.at[phase, p, way, m], to)

    def ring_start(phase, p, way, m):
        copy = ring_copy(phase, p, way, m)
        copy.start()
        pending.append(copy)

    def ring_send(phase, p, m):
        for way in range(2):
            ring_start(phase, p, way, m)

    def ring_first(phase, p):
        for m in range(2):
            ring_send(phase, p, m)

    def ring_add(phase, p):
        for way in range(2):
            ring_copy(phase, p, way, 0).wait_recv()
            near = 1 if way == 0 else 3
            if phase == 0:
                for h in range(2):
                    dw[p, near, way * 2 + h] = (
                        dw[p, near, way * 2 + h].astype(F32) + recv1[p, way, 0, h].astype(F32)
                    ).astype(BF16)
            else:
                here = pl.ds(way * 64, 64)
                zed[p, near, here] = (
                    zed[p, near, here].astype(F32) + recv2[p, way, 0].astype(F32)
                ).astype(BF16)
            ring_start(phase, p, way, 2)

    def ring_end(phase, p):
        for way in range(2):
            for m in range(1, 3):
                ring_copy(phase, p, way, m).wait_recv()
        for half in range(2):
            low_m, high_m = (2, 1) if half == 0 else (1, 2)
            if phase == 0:
                for h in range(2):
                    total = dw[p, 0, half * 2 + h].astype(F32)
                    total += recv1[p, 0, low_m, h].astype(F32)
                    total += recv1[p, 1, high_m, h].astype(F32)
                    zed[p, half * 2 + h] = total.astype(BF16)
            else:
                here = pl.ds(half * 64, 64)
                total = zed[p, 0, here].astype(F32)
                total += recv2[p, 0, low_m].astype(F32)
                total += recv2[p, 1, high_m].astype(F32)
                target = gate_ref if p < pieces // 2 else up_ref
                q = p % (pieces // 2)
                target[here, q * tile : (q + 1) * tile] = total.astype(BF16)
        if phase == 0:
            ring_first(1, p)

    def combine():
        for part in range(2):
            for j in range(1, NJ):
                back_copy(part, j).wait_recv()
        for group in range(3, -1, -1):
            rows = pl.ds(group * 16, 16)
            for n in range(0, dim, 512):
                cols = slice(n, n + 512)
                parts = jnp.concatenate(
                    [rows_back[0, rows, cols]] + [returned[j, rows, cols] for j in range(1, NJ)], 0
                )
                sums = lax.dot_general(pm[group], parts, over_tokens, preferred_element_type=F32)
                yown[group * 4 : group * 4 + 4, :, cols] = sums.reshape(4, tok, 512)

    wide = dim // 2

    def line_copy(way, hop, half):
        return remote(
            zsend.at[way, hop - 1, half], zrecv.at[way, hop - 1, half],
            z_send.at[way, hop - 1, half], z_recv.at[way, hop - 1, half],
            z_dev(-1 if way == 0 else 1),
        )

    def line_start(way, hop, half):
        copy = line_copy(way, hop, half)
        copy.start()
        pending.append(copy)

    def line_far():
        for way in range(2):
            zsend[way, HALF - 1, way] = yown[15, :, way * wide : (way + 1) * wide].astype(BF16)
            line_start(way, HALF, way)

    def line_step(hop):
        halves = ((1, 0), (0, 1)) if hop == HALF - 1 else ((0, 1), (0, 1))
        for turn_ in range(2):
            for way in range(2):
                half = halves[way][turn_] if hop == HALF - 1 else turn_
                total = yown[slot_of(way, hop), :, half * wide : (half + 1) * wide]
                if hop < HALF - 1 or half == way:
                    line_copy(way, hop + 1, half).wait_recv()
                    total = total + zrecv[way, hop, half].astype(F32)
                zsend[way, hop - 1, half] = total.astype(BF16)
                line_start(way, hop, half)

    def line_end():
        for half in range(2):
            cols = slice(half * wide, (half + 1) * wide)
            total = yown[12, :, cols]
            for way in range(2):
                line_copy(way, 1, half).wait_recv()
                total = total + zrecv[way, 0, half].astype(F32)
            out_ref[:, cols] = total.astype(BF16)

    do = functools.partial
    y_piece = thirds
    x_pieces = [p + half * thirds for p in range(thirds) for half in range(2)]
    x_pieces.remove(y_piece)

    def ready(f):
        weight_piece(f)
        if f == 0:
            ring_first(0, x_pieces[0])
        elif f == 1:
            ring_send(0, x_pieces[1], 0)
        weight_piece(f + thirds)

    def arrived():
        unpack_far()
        back_start(0)

    project(2, 4, arrived, ready)
    row_grads(1)
    back_start(1)
    ring_first(0, y_piece)
    step = 8.6
    tasks = [(26, do(ring_add, 0, y_piece)), (42, do(ring_end, 0, y_piece))]
    tasks += [(48, do(ring_add, 1, y_piece)), (54, do(ring_end, 1, y_piece))]
    for i, p in enumerate(x_pieces):
        when = step * i + 5
        tasks.append((when, do(ring_add, 0, p)))
        if i + 1 < len(x_pieces):
            tasks.append((when + 0.01, do(ring_send, 0, x_pieces[i + 1], 1)))
        if i + 2 < len(x_pieces):
            tasks.append((when + 0.02, do(ring_send, 0, x_pieces[i + 2], 0)))
        tasks.append((when + 9.6, do(ring_end, 0, p)))
        tasks.append((when + 15.6, do(ring_add, 1, p)))
        tasks.append((when + 23.6, do(ring_end, 1, p)))
    tasks.append((16, combine))
    tasks.append((16.1, line_far))
    for hop in range(HALF - 1, 0, -1):
        tasks.append((16.2 + 4.6 * (HALF - hop), do(line_step, hop)))
    tasks.append((16.2 + 4.6 * HALF, line_end))
    for _, task in sorted(tasks, key=lambda entry: entry[0]):
        task()
    for copy in pending:
        copy.wait_send()


def hand_on(a, b, c, a_out, b_out, c_out):
    a_out[...] = a[...]
    b_out[...] = b[...]
    c_out[...] = c[...]


def body(quant_rows, row_scales, out_grads, routes, probs, w_gate, w_up, w_down):
    tok, dim = quant_rows.shape
    ff = w_gate.shape[2]
    pieces = 2 * ff // 256
    vmem = pl.BlockSpec(memory_space=pltpu.VMEM)
    hbm = pl.BlockSpec(memory_space=pl.ANY)
    dma = pltpu.SemaphoreType.DMA
    wide = dim // 2
    out, gate, up = pl.pallas_call(
        kernel,
        out_shape=(
            jax.ShapeDtypeStruct((tok, dim), BF16),
            jax.ShapeDtypeStruct((128, ff), BF16),
            jax.ShapeDtypeStruct((128, ff), BF16),
        ),
        in_specs=[vmem] * 5 + [hbm] * 3,
        out_specs=(vmem, vmem, vmem),
        scratch_shapes=[
            pltpu.VMEM((dim, ff), BF16),
            pltpu.VMEM((dim, ff), BF16),
            pltpu.VMEM((ff, dim), BF16),
            pltpu.VMEM((NZ, 8, NJ * tok), F32),
            pltpu.VMEM((NZ, tok, dim), BF16),
            pltpu.VMEM((NZ, tok, dim), BF16),
            pltpu.VMEM((4, 64, NJ * tok), BF16),
            pltpu.VMEM((2, 4, NJ, 16, dim), BF16),
            pltpu.VMEM((2, 4, NJ, 16, dim), BF16),
            pltpu.VMEM((dim // 256, 256, 256), BF16),
            pltpu.VMEM((pieces, 256, 256), BF16),
            pltpu.VMEM((NJ, 64, dim), BF16),
            pltpu.VMEM((NJ, 64, dim), BF16),
            pltpu.VMEM((NZ, tok, dim), F32),
            pltpu.VMEM((2, HALF, 2, tok, wide), BF16),
            pltpu.VMEM((2, HALF, 2, tok, wide), BF16),
            pltpu.VMEM((pieces, 4, 4, 128, 256), BF16),
            pltpu.VMEM((pieces, 4, 128, 256), BF16),
            pltpu.VMEM((pieces, 2, 3, 2, 128, 256), BF16),
            pltpu.VMEM((pieces, 2, 3, 64, 256), BF16),
            pltpu.VMEM((2, 3, 16, dim // 4), BF16),
            pltpu.VMEM((2, 3, 16, dim // 4), BF16),
            dma((3,)),
            dma((2, HALF, SUBS)),
            dma((2, HALF, SUBS)),
            dma((4, 3, 2)),
            dma((4, 3, 2)),
            dma((2, 3)),
            dma((2, 3)),
            dma((2, HALF, 2)),
            dma((2, HALF, 2)),
            dma((2, pieces, 2, 3)),
            dma((2, pieces, 2, 3)),
            dma((3, 2)),
            dma((3, 2)),
        ],
        compiler_params=pltpu.CompilerParams(
            collective_id=0, has_side_effects=True, vmem_limit_bytes=60 * 1024 * 1024
        ),
    )(
        quant_rows, row_scales.reshape(1, tok), out_grads, routes.T, probs.T,
        w_gate[0], w_up[0], w_down[0],
    )
    out, gate, up = pl.pallas_call(
        hand_on,
        out_shape=tuple(jax.ShapeDtypeStruct(a.shape, a.dtype) for a in (out, gate, up)),
        in_specs=[vmem] * 3,
        out_specs=(vmem,) * 3,
    )(out, gate, up)
    return out, gate[None], up[None]


def solution(mesh):
    in_specs = (
        P(("rep", "exp"), None),
        P(("rep", "exp")),
        P(("rep", "exp"), None),
        P(("rep", "exp"), None),
        P(("rep", "exp"), None),
        P("exp", None, None),
        P("exp", None, None),
        P("exp", None, None),
    )
    out_specs = (P(("rep", "exp"), None), P("exp", "rep", None), P("exp", "rep", None))
    return jax.shard_map(body, mesh=mesh, in_specs=in_specs, out_specs=out_specs, check_vma=False)
```

```python
import functools

import jax
import jax.numpy as jnp
from jax import lax
from jax.experimental import pallas as pl
from jax.experimental.pallas import tpu as pltpu
from jax.sharding import PartitionSpec as P

MESH = pl.DeviceIdType.MESH
F32 = jnp.float32
BF16 = jnp.bfloat16

NX, NYH, NZ, NC = 4, 4, 16, 2
NJ = 4
HALF = NZ // 2
CAP = 4
SUBS = 3


def kernel(
    x_ref, scale_ref, g_ref, routes_ref, probs_ref, wg_hbm, wu_hbm, wd_hbm,
    out_ref, gate_ref, up_ref,
    wg, wu, wd, meta, xs, gs, pm, stage, got, xt, both, rows_back, returned, yown,
    zsend, zrecv, dw, zed, recv1, recv2, far_send, far_recv,
    w_sem, f_send, f_recv, p_send, p_recv, b_send, b_recv, z_send, z_recv, r_send, r_recv,
    q_send, q_recv,
):
    tok, dim = x_ref.shape
    ff = wg.shape[1]
    tile = 256
    pieces = 2 * ff // tile
    rep, exp = lax.axis_index("rep"), lax.axis_index("exp")
    my_x, my_y = rep // NYH, rep % NYH
    y_lo, z, core = exp // (NZ * NC), exp // NC % NZ, exp % NC

    def z_dev(step):
        return (rep, y_lo * (NZ * NC) + (z + NZ + step) % NZ * NC + core)

    def plane_exp(j):
        other_y = 1 - y_lo if j // 2 else y_lo
        other_c = 1 - core if j % 2 else core
        return other_y * (NZ * NC) + z * NC + other_c

    def x_dev(step):
        return ((my_x + NX + step) % NX * NYH + my_y, exp)

    def y_dev(step):
        return (my_x * NYH + (my_y + NYH + step) % NYH, exp)

    weights = [
        pltpu.make_async_copy(src, dst, w_sem.at[i])
        for i, (src, dst) in enumerate(((wg_hbm, wg), (wu_hbm, wu), (wd_hbm, wd)))
    ]
    for copy in weights:
        copy.start()

    neighbours = [z_dev(1), z_dev(-1), x_dev(1), x_dev(-1), y_dev(1), y_dev(-1)]
    neighbours += [(rep, plane_exp(j)) for j in range(1, NJ)]
    barrier = pltpu.get_barrier_semaphore()
    for device in neighbours:
        pl.semaphore_signal(barrier, inc=1, device_id=device, device_id_type=MESH)

    def iota(shape, axis):
        return lax.broadcasted_iota(jnp.int32, shape, axis)

    diag = jnp.where(iota((tok, tok), 0) == iota((tok, tok), 1), scale_ref[...].astype(F32), 0.0)
    diag = diag.astype(BF16)
    xs[12] = jnp.dot(diag, x_ref[...], preferred_element_type=F32).astype(BF16)
    gs[12] = g_ref[...]
    lanes = NJ * tok
    spread = (iota((tok, lanes), 1) % tok == iota((tok, lanes), 0)).astype(BF16)
    over_tokens = (((0,), (0,)), ((), ()))
    table = jnp.dot(
        routes_ref[...].astype(F32).astype(BF16), spread, preferred_element_type=F32
    )
    chance = jnp.dot(probs_ref[...], spread, preferred_element_type=F32)
    experts = NJ * NZ
    hits = [iota((experts, lanes), 0).astype(F32) == table[k : k + 1] for k in range(4)]
    named = sum(hit.astype(F32) for hit in hits)
    a, b = iota((lanes, lanes), 0), iota((lanes, lanes), 1)
    before = ((a // tok == b // tok) & (a < b)).astype(BF16)
    rank = jnp.dot(named.astype(BF16), before, preferred_element_type=F32)
    for k in range(4):
        mine = jnp.sum(jnp.where(hits[k], rank, 0.0), axis=0, keepdims=True)
        meta[12, k : k + 1, :] = table[k : k + 1] * CAP + mine
        meta[12, 4 + k : 5 + k, :] = chance[k : k + 1]

    pl.semaphore_wait(barrier, len(neighbours))

    pending = []

    def remote(src, dst, send, recv, device):
        return pltpu.make_async_remote_copy(
            src_ref=src, dst_ref=dst, send_sem=send, recv_sem=recv,
            device_id=device, device_id_type=MESH,
        )

    travels = (meta, xs, gs)

    def slot_of(way, hop):
        near = {0: 12, 1: 13 + way, HALF: 15}
        return near[hop] if hop in near else 2 * (hop - 2) + way

    def carries(way, hop, sub):
        return hop < HALF or (sub == 2) == (way == 1)

    def hop_copy(way, hop, sub):
        buf = travels[sub]
        return remote(
            buf.at[slot_of(way, hop - 1)], buf.at[slot_of(way, hop)],
            f_send.at[way, hop - 1, sub], f_recv.at[way, hop - 1, sub],
            z_dev(1 if way == 0 else -1),
        )

    def hop_start(way, hop, sub):
        if hop <= HALF and carries(way, hop, sub):
            copy = hop_copy(way, hop, sub)
            copy.start()
            pending.append(copy)

    for sub in range(SUBS):
        for way in range(2):
            hop_start(way, 1, sub)

    group_rows = NJ * 4 * CAP
    r = iota((group_rows, lanes), 0)
    c = iota((group_rows, lanes), 1)
    expert_of = jnp.where(
        r // 16 == 0, plane_exp(0),
        jnp.where(r // 16 == 1, plane_exp(1), jnp.where(r // 16 == 2, plane_exp(2), plane_exp(3))),
    )
    slot_id = jnp.where(r % 16 // CAP == c // tok, expert_of * CAP + r % CAP, -1).astype(F32)

    def plane_copy(group, j, kind):
        return remote(
            stage.at[kind, group, j], got.at[kind, group, j],
            p_send.at[group, j - 1, kind], p_recv.at[group, j - 1, kind], (rep, plane_exp(j)),
        )

    def picks(group):
        lane_group = iota((8, lanes), 1) // tok
        mix = meta[group * 4]
        for m in range(1, 4):
            mix = jnp.where(lane_group == m, meta[group * 4 + m], mix)
        hit = [slot_id == mix[k : k + 1] for k in range(4)]
        ones = sum(h.astype(F32) for h in hit)
        weighed = sum(jnp.where(hit[k], mix[4 + k : 5 + k], 0.0) for k in range(4))
        return ones.astype(BF16), weighed.astype(BF16)

    def select(group, kind):
        members = 4 if group < 3 else 3
        pick = picks(group)
        if kind == 0:
            pm[group] = pick[0]
        chosen_of = pick[kind][:, : members * tok]
        buf = travels[1 + kind]
        for n in range(0, dim, 512):
            block = buf[group * 4 : group * 4 + members, :, n : n + 512]
            block = block.reshape(members * tok, 512)
            chosen = jnp.dot(chosen_of, block, preferred_element_type=F32).astype(BF16)
            got[kind, group, 0, :, n : n + 512] = chosen[:16]
            stage[kind, group, 1:, :, n : n + 512] = chosen[16:].reshape(3, 16, 512)
        for j in range(1, NJ):
            copy = plane_copy(group, j, kind)
            copy.start()
            pending.append(copy)

    quarter = dim // 4

    def far_copy(j, kind):
        return remote(
            far_send.at[kind, j - 1], far_recv.at[kind, j - 1],
            q_send.at[j - 1, kind], q_recv.at[j - 1, kind], (rep, plane_exp(j)),
        )

    def far_picks(slot):
        last = meta[15][:, :tok]
        hit = [slot == last[k : k + 1] for k in range(4)]
        ones = sum(h.astype(F32) for h in hit)
        weighed = sum(jnp.where(hit[k], last[4 + k : 5 + k], 0.0) for k in range(4))
        return ones, weighed

    def select_far():
        pm[3] = picks(3)[0]
        row = iota((48, tok), 0)
        owner = jnp.where(
            row // 16 == 0, plane_exp(1), jnp.where(row // 16 == 1, plane_exp(2), plane_exp(3))
        )
        sent = far_picks((owner * CAP + row % CAP).astype(F32))
        for kind in range(2):
            buf = travels[1 + kind]
            total = jnp.zeros((48, quarter), F32)
            for q in range(4):
                pick = jnp.where(row % 16 // CAP == q, sent[kind], 0.0).astype(BF16)
                block = buf[15, :, q * quarter : (q + 1) * quarter]
                total += jnp.dot(pick, block, preferred_element_type=F32)
            far_send[kind] = total.astype(BF16).reshape(3, 16, quarter)
            for j in range(1, NJ):
                copy = far_copy(j, kind)
                copy.start()
                pending.append(copy)
        row = iota((16, tok), 0)
        slot = jnp.where(row // CAP == 3, plane_exp(0) * CAP + row % CAP, -1)
        kept = far_picks(slot.astype(F32))
        for kind in range(2):
            buf = travels[1 + kind]
            for n in range(0, dim, 512):
                cols = slice(n, n + 512)
                more = jnp.dot(
                    kept[kind].astype(BF16), buf[15, :, cols], preferred_element_type=F32
                )
                got[kind, 3, 0, :, cols] = (got[kind, 3, 0, :, cols].astype(F32) + more).astype(BF16)

    def unpack_far():
        a, b = iota((48, 48), 0), iota((48, 48), 1)
        same = (a // 16 == b // 16) & (a % 16 // CAP == 3) & (a % CAP == b % CAP)
        for kind in range(2):
            for j in range(1, NJ):
                far_copy(j, kind).wait_recv()
            packed = far_recv[kind].reshape(48, quarter)
            for q in range(4):
                cols = slice(q * quarter, (q + 1) * quarter)
                place = (same & (b % 16 // CAP == q)).astype(F32).astype(BF16)
                more = jnp.dot(place, packed, preferred_element_type=F32)
                old = got[kind, 3, 1:, :, cols].reshape(48, quarter).astype(F32)
                got[kind, 3, 1:, :, cols] = (old + more).astype(BF16).reshape(3, 16, quarter)

    slots = NJ * 64
    over_last = (((1,), (1,)), ((), ()))

    def project(low, high, arrived=None, ready=None):
        for group in range(low, high):
            for j in range(1, NJ):
                for kind in range(2):
                    plane_copy(group, j, kind).wait_recv()
        if arrived is not None:
            arrived()
        here, count = slice(low * 64, high * 64), (high - low) * 64
        for n in range(dim // tile):
            block = got[0, low:high, :, :, n * tile : (n + 1) * tile]
            xt[n, :, here] = block.reshape(count, tile).T
        for f in range(ff // tile):
            cols = slice(f * tile, (f + 1) * tile)
            ins = got[0, low:high].reshape(count, dim)
            gate = jnp.dot(ins, wg[:, cols], preferred_element_type=F32)
            up = jnp.dot(ins, wu[:, cols], preferred_element_type=F32)
            grads = got[1, low:high].reshape(count, dim)
            hidden = lax.dot_general(grads, wd[cols, :], over_last, preferred_element_type=F32)
            s = jax.nn.sigmoid(gate)
            both[f, here] = (hidden * up * s * (1.0 + gate * (1.0 - s))).astype(BF16)
            both[f + ff // tile, here] = (hidden * gate * s).astype(BF16)
            if ready is not None:
                ready(f)

    def back_copy(part, j):
        rows = pl.ds(part * 32, 32)
        return remote(
            rows_back.at[j, rows], returned.at[j, rows],
            b_send.at[part, j - 1], b_recv.at[part, j - 1], (rep, plane_exp(j)),
        )

    def row_grads(part):
        low, high = ((0, 2), (2, 4))[part]
        here, count = slice(low * 64, high * 64), (high - low) * 64

        def one(n, carry):
            cols = pl.ds(pl.multiple_of(n * tile, tile), tile)
            total = jnp.zeros((count, tile), F32)
            for k in range(ff // tile):
                inner = slice(k * tile, (k + 1) * tile)
                total += lax.dot_general(
                    both[k, here], wg[cols, inner], over_last, preferred_element_type=F32
                )
                total += lax.dot_general(
                    both[k + ff // tile, here], wu[cols, inner], over_last,
                    preferred_element_type=F32,
                )
            value = total.astype(BF16).reshape(high - low, NJ, 16, tile)
            for j in range(NJ):
                rows = slice(low * 16, high * 16)
                rows_back[j, rows, cols] = value[:, j].reshape(count // NJ, tile)
            return carry

        lax.fori_loop(0, dim // tile, one, 0)

    def back_start(part):
        for j in range(1, NJ):
            copy = back_copy(part, j)
            copy.start()
            pending.append(copy)

    group_at = {1: 3, 3: 0, 5: 1, 7: 2}
    for hop in range(1, HALF + 1):
        for sub in range(SUBS):
            for way in range(2):
                if carries(way, hop, sub):
                    hop_copy(way, hop, sub).wait_recv()
                    hop_start(way, hop + 1, sub)
            if hop in group_at and sub > 0:
                select(group_at[hop], sub - 1)
        if hop == 2:
            for copy in weights:
                copy.wait()
        if hop >= 6 and hop < HALF:
            project(hop - 6, hop - 5)
    select_far()
    row_grads(0)

    axes = ((x_dev, y_dev), (y_dev, x_dev))
    thirds = ff // tile
    order_of = [1 if p == thirds else 0 for p in range(pieces)]

    def weight_piece(p):
        order = order_of[p]

        for i in range(dim // tile):
            value = jnp.dot(xt[i], both[p], preferred_element_type=F32).astype(BF16)
            rx = (i // 2 - my_x + NX) % NX
            for h in range(2):
                ry = (2 * (i % 2) + h - my_y + NYH) % NYH
                part = value[h * 128 : (h + 1) * 128]
                if order == 0:
                    dw[p, rx, ry] = part
                else:
                    dw[p, ry, rx] = part

    def ring_copy(phase, p, way, m):
        to = axes[order_of[p]][phase](1 if way == 0 else -1)
        near = 1 if way == 0 else 3
        block = (2, near, near)[m]
        half = (way, 1 - way, way)[m]
        if phase == 0:
            src = dw.at[p, block, pl.ds(half * 2, 2)]
            dst = recv1.at[p, way, m]
        else:
            src = zed.at[p, block, pl.ds(half * 64, 64)]
            dst = recv2.at[p, way, m]
        return remote(src, dst, r_send.at[phase, p, way, m], r_recv.at[phase, p, way, m], to)

    def ring_start(phase, p, way, m):
        copy = ring_copy(phase, p, way, m)
        copy.start()
        pending.append(copy)

    def ring_send(phase, p, m):
        for way in range(2):
            ring_start(phase, p, way, m)

    def ring_first(phase, p):
        for m in range(2):
            ring_send(phase, p, m)

    def ring_add(phase, p):
        for way in range(2):
            ring_copy(phase, p, way, 0).wait_recv()
            near = 1 if way == 0 else 3
            if phase == 0:
                for h in range(2):
                    dw[p, near, way * 2 + h] = (
                        dw[p, near, way * 2 + h].astype(F32) + recv1[p, way, 0, h].astype(F32)
                    ).astype(BF16)
            else:
                here = pl.ds(way * 64, 64)
                zed[p, near, here] = (
                    zed[p, near, here].astype(F32) + recv2[p, way, 0].astype(F32)
                ).astype(BF16)
            ring_start(phase, p, way, 2)

    def ring_end(phase, p):
        for way in range(2):
            for m in range(1, 3):
                ring_copy(phase, p, way, m).wait_recv()
        for half in range(2):
            low_m, high_m = (2, 1) if half == 0 else (1, 2)
            if phase == 0:
                for h in range(2):
                    total = dw[p, 0, half * 2 + h].astype(F32)
                    total += recv1[p, 0, low_m, h].astype(F32)
                    total += recv1[p, 1, high_m, h].astype(F32)
                    zed[p, half * 2 + h] = total.astype(BF16)
            else:
                here = pl.ds(half * 64, 64)
                total = zed[p, 0, here].astype(F32)
                total += recv2[p, 0, low_m].astype(F32)
                total += recv2[p, 1, high_m].astype(F32)
                target = gate_ref if p < pieces // 2 else up_ref
                q = p % (pieces // 2)
                target[here, q * tile : (q + 1) * tile] = total.astype(BF16)
        if phase == 0:
            ring_first(1, p)

    def combine():
        for part in range(2):
            for j in range(1, NJ):
                back_copy(part, j).wait_recv()
        for group in range(3, -1, -1):
            rows = pl.ds(group * 16, 16)
            for n in range(0, dim, 512):
                cols = slice(n, n + 512)
                parts = jnp.concatenate(
                    [rows_back[0, rows, cols]] + [returned[j, rows, cols] for j in range(1, NJ)], 0
                )
                sums = lax.dot_general(pm[group], parts, over_tokens, preferred_element_type=F32)
                yown[group * 4 : group * 4 + 4, :, cols] = sums.reshape(4, tok, 512)

    wide = dim // 2

    def line_copy(way, hop, half):
        return remote(
            zsend.at[way, hop - 1, half], zrecv.at[way, hop - 1, half],
            z_send.at[way, hop - 1, half], z_recv.at[way, hop - 1, half],
            z_dev(-1 if way == 0 else 1),
        )

    def line_start(way, hop, half):
        copy = line_copy(way, hop, half)
        copy.start()
        pending.append(copy)

    def line_far():
        for way in range(2):
            zsend[way, HALF - 1, way] = yown[15, :, way * wide : (way + 1) * wide].astype(BF16)
            line_start(way, HALF, way)

    def line_step(hop):
        halves = ((1, 0), (0, 1)) if hop == HALF - 1 else ((0, 1), (0, 1))
        for turn_ in range(2):
            for way in range(2):
                half = halves[way][turn_] if hop == HALF - 1 else turn_
                total = yown[slot_of(way, hop), :, half * wide : (half + 1) * wide]
                if hop < HALF - 1 or half == way:
                    line_copy(way, hop + 1, half).wait_recv()
                    total = total + zrecv[way, hop, half].astype(F32)
                zsend[way, hop - 1, half] = total.astype(BF16)
                line_start(way, hop, half)

    def line_end():
        for half in range(2):
            cols = slice(half * wide, (half + 1) * wide)
            total = yown[12, :, cols]
            for way in range(2):
                line_copy(way, 1, half).wait_recv()
                total = total + zrecv[way, 0, half].astype(F32)
            out_ref[:, cols] = total.astype(BF16)

    do = functools.partial
    y_piece = thirds
    x_pieces = [p + half * thirds for p in range(thirds) for half in range(2)]
    x_pieces.remove(y_piece)

    def ready(f):
        weight_piece(f)
        if f == 0:
            ring_first(0, x_pieces[0])
        elif f == 1:
            ring_send(0, x_pieces[1], 0)
        weight_piece(f + thirds)

    def arrived():
        unpack_far()
        back_start(0)

    project(2, 4, arrived, ready)
    row_grads(1)
    back_start(1)
    ring_first(0, y_piece)
    step = 8.6
    tasks = [(26, do(ring_add, 0, y_piece)), (42, do(ring_end, 0, y_piece))]
    tasks += [(48, do(ring_add, 1, y_piece)), (54, do(ring_end, 1, y_piece))]
    for i, p in enumerate(x_pieces):
        when = step * i + 5
        tasks.append((when, do(ring_add, 0, p)))
        if i + 1 < len(x_pieces):
            tasks.append((when + 0.01, do(ring_send, 0, x_pieces[i + 1], 1)))
        if i + 2 < len(x_pieces):
            tasks.append((when + 0.02, do(ring_send, 0, x_pieces[i + 2], 0)))
        tasks.append((when + 9.6, do(ring_end, 0, p)))
        tasks.append((when + 15.6, do(ring_add, 1, p)))
        tasks.append((when + 23.6, do(ring_end, 1, p)))
    tasks.append((20, combine))
    tasks.append((20.1, line_far))
    for hop in range(HALF - 1, 0, -1):
        tasks.append((20.2 + 4.2 * (HALF - hop), do(line_step, hop)))
    tasks.append((20.2 + 4.2 * HALF, line_end))
    for _, task in sorted(tasks, key=lambda entry: entry[0]):
        task()
    for copy in pending:
        copy.wait_send()


def hand_on(a, b, c, a_out, b_out, c_out):
    a_out[...] = a[...]
    b_out[...] = b[...]
    c_out[...] = c[...]


def body(quant_rows, row_scales, out_grads, routes, probs, w_gate, w_up, w_down):
    tok, dim = quant_rows.shape
    ff = w_gate.shape[2]
    pieces = 2 * ff // 256
    vmem = pl.BlockSpec(memory_space=pltpu.VMEM)
    hbm = pl.BlockSpec(memory_space=pl.ANY)
    dma = pltpu.SemaphoreType.DMA
    wide = dim // 2
    out, gate, up = pl.pallas_call(
        kernel,
        out_shape=(
            jax.ShapeDtypeStruct((tok, dim), BF16),
            jax.ShapeDtypeStruct((128, ff), BF16),
            jax.ShapeDtypeStruct((128, ff), BF16),
        ),
        in_specs=[vmem] * 5 + [hbm] * 3,
        out_specs=(vmem, vmem, vmem),
        scratch_shapes=[
            pltpu.VMEM((dim, ff), BF16),
            pltpu.VMEM((dim, ff), BF16),
            pltpu.VMEM((ff, dim), BF16),
            pltpu.VMEM((NZ, 8, NJ * tok), F32),
            pltpu.VMEM((NZ, tok, dim), BF16),
            pltpu.VMEM((NZ, tok, dim), BF16),
            pltpu.VMEM((4, 64, NJ * tok), BF16),
            pltpu.VMEM((2, 4, NJ, 16, dim), BF16),
            pltpu.VMEM((2, 4, NJ, 16, dim), BF16),
            pltpu.VMEM((dim // 256, 256, 256), BF16),
            pltpu.VMEM((pieces, 256, 256), BF16),
            pltpu.VMEM((NJ, 64, dim), BF16),
            pltpu.VMEM((NJ, 64, dim), BF16),
            pltpu.VMEM((NZ, tok, dim), F32),
            pltpu.VMEM((2, HALF, 2, tok, wide), BF16),
            pltpu.VMEM((2, HALF, 2, tok, wide), BF16),
            pltpu.VMEM((pieces, 4, 4, 128, 256), BF16),
            pltpu.VMEM((pieces, 4, 128, 256), BF16),
            pltpu.VMEM((pieces, 2, 3, 2, 128, 256), BF16),
            pltpu.VMEM((pieces, 2, 3, 64, 256), BF16),
            pltpu.VMEM((2, 3, 16, dim // 4), BF16),
            pltpu.VMEM((2, 3, 16, dim // 4), BF16),
            dma((3,)),
            dma((2, HALF, SUBS)),
            dma((2, HALF, SUBS)),
            dma((4, 3, 2)),
            dma((4, 3, 2)),
            dma((2, 3)),
            dma((2, 3)),
            dma((2, HALF, 2)),
            dma((2, HALF, 2)),
            dma((2, pieces, 2, 3)),
            dma((2, pieces, 2, 3)),
            dma((3, 2)),
            dma((3, 2)),
        ],
        compiler_params=pltpu.CompilerParams(
            collective_id=0, has_side_effects=True, vmem_limit_bytes=60 * 1024 * 1024
        ),
    )(
        quant_rows, row_scales.reshape(1, tok), out_grads, routes.T, probs.T,
        w_gate[0], w_up[0], w_down[0],
    )
    out, gate, up = pl.pallas_call(
        hand_on,
        out_shape=tuple(jax.ShapeDtypeStruct(a.shape, a.dtype) for a in (out, gate, up)),
        in_specs=[vmem] * 3,
        out_specs=(vmem,) * 3,
    )(out, gate, up)
    return out, gate[None], up[None]


def solution(mesh):
    in_specs = (
        P(("rep", "exp"), None),
        P(("rep", "exp")),
        P(("rep", "exp"), None),
        P(("rep", "exp"), None),
        P(("rep", "exp"), None),
        P("exp", None, None),
        P("exp", None, None),
        P("exp", None, None),
    )
    out_specs = (P(("rep", "exp"), None), P("exp", "rep", None), P("exp", "rep", None))
    return jax.shard_map(body, mesh=mesh, in_specs=in_specs, out_specs=out_specs, check_vma=False)
```
